256 devices in a mesh: bond: 32 (over x, y, core), mpo: 8 (over z).
Axes of the slice: x: 4, y: 4, z: 8, core: 2. Of those that a mesh axis runs over, the one named last changes fastest.
Arguments:
- wavefunction: bfloat16 [16, 1024, 1024], P(None, 'bond'), may hold values from -6 to 6
- left_env: bfloat16 [24, 32, 512, 1024], P('mpo', 'bond'), may hold values from -0.0390625 to 0.0390625
- right_env: bfloat16 [24, 32, 512, 1024], P('mpo', 'bond'), may hold values from -0.1875 to 0.1875
- left_sizes: int32 [16], replicated, may hold values from 512 to 1024, as said below
- right_sizes: int32 [16], replicated, may hold values from 512 to 1024, as said below
- channel_shift: int32 [24], replicated, may hold values from -1 to 1, as said below
Outputs:
- first_step: bfloat16 [16, 1024, 1024], P(None, 'bond', 'mpo')
- second_step: bfloat16 [16, 1024, 1024], P(None, 'bond', 'mpo')
The draws below stay inside these ranges and needn't reach their ends.
Inputs may be any that keep to these rules, and one draw needn't show every extreme that they name: `left_sizes`: some sector has exactly 1024 left states. `right_sizes`: some sector has exactly 1024 right states. `channel_shift`: each aligned block of 3 consecutive channels holds -1, 0 and 1 once each.
All inputs are finite; a program needn't handle non-finite values.
Results may differ from the reference program's by a relative error of at most 0.025.
Values may be sent and summed in bfloat16 or wider, within the bound.
A program may use at most 128 MiB of HBM per device.

```python
import jax
import jax.numpy as jnp
from jax import lax

S = 1024
W = 24
K = 16
HALF = 16
N_BOND = 32
N_MPO = 8


def sector_sizes(key):
    values = jax.random.randint(key, (K,), S // 2, S + 1, dtype=jnp.int32)
    widest = jax.random.randint(jax.random.fold_in(key, 7), (), 0, K, dtype=jnp.int32)
    return jnp.where(jnp.arange(K, dtype=jnp.int32) == widest, S, values).astype(jnp.int32)


def draw_left_sizes(key, part):
    key = jax.random.fold_in(key, 11)
    return sector_sizes(key)


def draw_right_sizes(key, part):
    key = jax.random.fold_in(key, 12)
    return sector_sizes(key)


def block_order(subkey):
    return jax.random.permutation(subkey, 3)


def draw_channel_shift(key, part):
    key = jax.random.fold_in(key, 13)
    subkeys = jax.random.split(key, W // 3)
    orders = jax.vmap(block_order)(subkeys)
    return (orders.reshape(W) - 1).astype(jnp.int32)


def level_of(own_key, shape, cuts, smallest, top_value):
    def one(dim, shards_of):
        heights = jax.random.uniform(jax.random.fold_in(jax.random.fold_in(own_key, 6), dim), (shards_of,), jnp.float32, smallest / len(cuts), top_value / len(cuts))
        return jnp.repeat(jnp.exp(heights), shape[dim] // shards_of).reshape((-1,) + (1,) * (len(shape) - dim - 1))

    loudness = one(*cuts[0])
    for cut in cuts[1:]:
        loudness = loudness * one(*cut)
    return loudness


def bell_draw(rng, shape, spread, limit, shards=(), held_as=jnp.bfloat16):
    factor_of = level_of(rng, shape, shards, -0.22, 0.18) if shards else 1.0
    result = jax.random.normal(rng, shape, jnp.float32) * spread * factor_of
    return jnp.minimum(jnp.maximum(result, -limit), limit).astype(held_as)


def setup_inputs(seed: int = 0) -> dict:
    key_list = jax.random.split(jax.random.key(seed), 7)
    wavefunction = bell_draw(key_list[0], (K, S, S), 1.0, 6.0, ((1, 32),))
    left_env = bell_draw(key_list[1], (W, 2 * K, S // 2, S), (S * W) ** -0.5, 0.0390625, ((0, 8), (1, 32)))
    right_env = bell_draw(key_list[2], (W, 2 * K, S // 2, S), S ** -0.5, 0.1875, ((0, 8), (1, 32)))
    left_sizes = draw_left_sizes(jax.random.fold_in(key_list[6], 71), 0)
    right_sizes = draw_right_sizes(jax.random.fold_in(key_list[6], 71), 0)
    channel_shift = draw_channel_shift(jax.random.fold_in(key_list[6], 71), 0)
    return dict(wavefunction=wavefunction, left_env=left_env, right_env=right_env, left_sizes=left_sizes, right_sizes=right_sizes, channel_shift=channel_shift)


def unpack_env(environment):
    channels = environment.shape[0]
    blocks = environment.reshape(channels, K, 2, N_BOND, HALF, S)
    blocks = jnp.transpose(blocks, (0, 1, 3, 2, 4, 5))
    return blocks.reshape(channels, K, S, S)


def shift_sectors(values, offset):
    zero_block = jnp.zeros_like(values[:1])
    if offset > 0:
        return jnp.concatenate((zero_block, values[:-1]), axis=0)
    return jnp.concatenate((values[1:], zero_block), axis=0)


def apply_hamiltonian(vector, left_blocks, right_blocks, channel_shift, live_mask):
    group_size = W // N_MPO
    vector32 = vector.astype(jnp.float32)

    def group_step(index, total):
        def channel_step(carry, offset):
            channel = index * group_size + offset
            left = lax.dynamic_index_in_dim(left_blocks, channel, 0, keepdims=False).astype(jnp.float32)
            right = lax.dynamic_index_in_dim(right_blocks, channel, 0, keepdims=False).astype(jnp.float32)
            mixed = jnp.einsum("qij,qjk->qik", left, vector32).astype(jnp.bfloat16)
            mixed = lax.optimization_barrier(mixed).astype(jnp.float32)
            product = jnp.einsum("qik,qlk->qil", mixed, right)
            shift_now = channel_shift[channel]
            lower_sum = carry[0] + jnp.where(shift_now == -1, product, 0.0)
            still_sum = carry[1] + jnp.where(shift_now == 0, product, 0.0)
            upper_sum = carry[2] + jnp.where(shift_now == 1, product, 0.0)
            return (lower_sum, still_sum, upper_sum), None

        zeros = jnp.zeros((K, S, S), jnp.float32)
        sums, unused = lax.scan(channel_step, (zeros, zeros, zeros), jnp.arange(group_size, dtype=jnp.int32))
        lower_part = lax.optimization_barrier(sums[0].astype(jnp.bfloat16)).astype(jnp.float32)
        upper_part = lax.optimization_barrier(sums[2].astype(jnp.bfloat16)).astype(jnp.float32)
        return total + sums[1] + shift_sectors(lower_part, -1) + shift_sectors(upper_part, 1)

    total = lax.fori_loop(0, N_MPO, group_step, jnp.zeros((K, S, S), jnp.float32))
    return jnp.where(live_mask, total, 0.0)


def reference(wavefunction, left_env, right_env, left_sizes, right_sizes, channel_shift):
    positions = jnp.arange(S, dtype=jnp.int32)
    live_mask = (positions[None, :, None] < left_sizes[:, None, None]) & (positions[None, None, :] < right_sizes[:, None, None])
    initial = jnp.where(live_mask, wavefunction, jnp.zeros((), wavefunction.dtype))
    left_blocks = unpack_env(left_env)
    right_blocks = unpack_env(right_env)
    first_step = apply_hamiltonian(initial, left_blocks, right_blocks, channel_shift, live_mask).astype(jnp.bfloat16)
    second_raw = apply_hamiltonian(first_step, left_blocks, right_blocks, channel_shift, live_mask)
    second_step = (2.0 * second_raw - initial.astype(jnp.float32)).astype(jnp.bfloat16)
    return (first_step, second_step)
```

```python
import jax
import jax.numpy as jnp
from jax import lax
from jax.experimental import pallas as pl
from jax.experimental.pallas import tpu as pltpu
from jax.sharding import PartitionSpec as P

MESH = pl.DeviceIdType.MESH
PIECES = 2


def kernel(
    wave,
    left_env,
    right_env,
    left_sizes,
    right_sizes,
    channel_shift,
    first_out,
    second_out,
    left,
    right,
    start_in,
    full,
    mixed,
    near,
    moved_out,
    moved_in,
    part_out,
    part_in,
    last,
    local_sem,
    pair_sem,
    scatter_sem,
    ring_send,
    ring_recv,
    cross_send,
    cross_recv,
    moved_send,
    moved_recv,
    part_send,
    part_recv,
    back_send,
    back_recv,
):
    bonds = lax.axis_size("bond")
    groups = lax.axis_size("mpo")
    me = lax.axis_index("bond")
    z = lax.axis_index("mpo")
    sectors = bonds // 2
    q = me // 2
    h = me % 2
    half = wave.shape[1] // 2
    rows = bonds * half
    cols = full.shape[-1]
    per_chunk = right.shape[1] // groups
    lines = bonds // PIECES
    piece_rows = rows // PIECES
    turn = 1 - 2 * h
    partner = (me + turn, z)
    ahead = (me, (z + turn + groups) % groups)
    behind = (me, (z - turn + groups) % groups)
    hops = groups // 2

    def chunk_at(offset):
        return (z + turn * offset + groups) % groups

    def remote(source, target, send, recv, device):
        return pltpu.make_async_remote_copy(
            src_ref=source,
            dst_ref=target,
            send_sem=send,
            recv_sem=recv,
            device_id=device,
            device_id_type=MESH,
        )

    right_own = right.at[:, :, h]
    load_left = pltpu.make_async_copy(left_env, left, local_sem.at[0])
    load_right = pltpu.make_async_copy(right_env, right_own, local_sem.at[1])
    load_left.start()
    load_right.start()

    barrier = pltpu.get_barrier_semaphore()

    def greet(i, carry):
        pl.semaphore_signal(
            barrier, inc=1, device_id=((me + i) % bonds, z), device_id_type=MESH
        )
        return carry

    pl.semaphore_signal(barrier, inc=1, device_id=ahead, device_id_type=MESH)
    pl.semaphore_signal(barrier, inc=1, device_id=behind, device_id_type=MESH)
    lax.fori_loop(1, bonds, greet, 0)
    pl.semaphore_wait(barrier, bonds + 1)

    my_cols = pl.ds(pl.multiple_of(z * cols, cols), cols)

    def piece_of_wave(p):
        return wave.at[p // 2, pl.ds(pl.multiple_of((p % 2) * half, half), half), my_cols]

    def scatter(i, carry):
        p = (me + i) % bonds
        remote(
            piece_of_wave(p), start_in.at[me], scatter_sem.at[0], scatter_sem.at[1], (p, z)
        ).start()
        return carry

    lax.fori_loop(1, bonds, scatter, 0)
    keep = pltpu.make_async_copy(piece_of_wave(me), start_in.at[me], local_sem.at[2])
    keep.start()
    others = start_in.at[pl.ds(0, bonds - 1)]

    @pl.when(q == 0)
    def _():
        for step in range(2):
            moved_in[step, 0] = jnp.zeros(moved_in.shape[2:], moved_in.dtype)

    @pl.when(q == sectors - 1)
    def _():
        for step in range(2):
            moved_in[step, 1] = jnp.zeros(moved_in.shape[2:], moved_in.dtype)

    row = lax.broadcasted_iota(jnp.int32, (rows, cols), 0)
    col = lax.broadcasted_iota(jnp.int32, (rows, cols), 1)
    row = (row // half) * (2 * half) + h * half + row % half
    live = (row < left_sizes[q]) & (col + z * cols < right_sizes[q])

    channels = left.shape[0]

    def channel_of(shift):
        found = channels - 1
        for j in range(channels - 1):
            found = jnp.where(channel_shift[z * channels + j] == shift, j, found)
        return found

    order = [channel_of(1), channel_of(-1), channel_of(0)]

    keep.wait()
    remote(others, others, scatter_sem.at[0], scatter_sem.at[1], partner).wait()
    initial = jnp.where(live, start_in[...].reshape(rows, cols), jnp.zeros((), start_in.dtype))
    full[0, z, :, h] = initial.reshape(bonds, half, cols)

    load_right.wait()
    swap_right = remote(right_own, right_own, pair_sem.at[0], pair_sem.at[1], partner)

    def apply(step, carry):
        def line_set(chunk, piece):
            return full.at[step, chunk, pl.ds(piece * lines, lines), h]

        def pass_on(chunk, slot, piece, device):
            block = line_set(chunk, piece)
            return remote(
                block, block, ring_send.at[step], ring_recv.at[step, slot, piece], device
            )

        def share(chunk, piece):
            block = line_set(chunk, piece)
            return remote(
                block, block, cross_send.at[step], cross_recv.at[step, chunk, piece], partner
            )

        def mix(chunks):
            vector = []
            for chunk in chunks:
                for piece in range(PIECES):
                    share(chunk, piece).wait_recv()
                vector.append(full[step, chunk].reshape(2 * rows, cols))
            vector = vector[0] if len(vector) == 1 else jnp.concatenate(vector, axis=1)
            for d in range(channels):
                block = jnp.dot(
                    left[order[d]], vector, preferred_element_type=jnp.float32
                ).astype(mixed.dtype)
                for n, chunk in enumerate(chunks):
                    mixed[d, :, pl.ds(pl.multiple_of(chunk * cols, cols), cols)] = block[
                        :, n * cols : (n + 1) * cols
                    ]

        for piece in range(PIECES):
            pass_on(z, 0, piece, ahead).start()
            pass_on(z, 1, piece, behind).start()
        for piece in range(PIECES):
            share(z, piece).start()

        @pl.when(step == 0)
        def _():
            swap_right.start()
            load_left.wait()

        @pl.when(step == 1)
        def _():
            send_back(first_out, full.at[1, z, :, h], 0)

        pending = [z]
        for s in range(1, hops + 1):
            from_behind, from_ahead = chunk_at(-s), chunk_at(s)
            now = [from_behind]
            if s < hops:
                now.append(from_ahead)
            for piece in range(PIECES):
                pass_on(from_behind, 2 * s - 2, piece, ahead).wait_recv()
                if s < hops:
                    pass_on(from_behind, 2 * s, piece, ahead).start()
                share(from_behind, piece).start()
                if s < hops:
                    pass_on(from_ahead, 2 * s - 1, piece, behind).wait_recv()
                    if s < hops - 1:
                        pass_on(from_ahead, 2 * s + 1, piece, behind).start()
                    share(from_ahead, piece).start()
            mix(pending)
            pending = now
        mix(pending)

        @pl.when(step == 0)
        def _():
            swap_right.wait()

        def order_of(k):
            distance = hops - (k + 1) // 2
            return chunk_at(distance * (1 - 2 * (k % 2)))

        def image(d, chunk):
            block = right[order[d], pl.ds(chunk * per_chunk, per_chunk)]
            return lax.dot_general(
                mixed[d],
                block.reshape(cols, block.shape[-1]),
                (((1,), (1,)), ((), ())),
                preferred_element_type=jnp.float32,
            )

        def to_sector(d, chunk, k, device=partner):
            return remote(
                moved_out.at[d, chunk],
                moved_in.at[step, d, chunk],
                moved_send.at[d],
                moved_recv.at[step, d, k],
                device,
            )

        has_target = [q < sectors - 1, q > 0]
        has_source = [q > 0, q < sectors - 1]

        def moved_chunk(k, inner):
            chunk = order_of(k)
            for d in range(2):
                moved_out[d, chunk] = image(d, chunk).astype(moved_out.dtype)

                @pl.when(has_target[d])
                def _():
                    to_sector(d, chunk, k, (me + (2 if d == 0 else -2), z)).start()

            return inner

        def near_chunk(k, inner):
            chunk = order_of(k)
            near[chunk] = image(2, chunk)
            return inner

        lax.fori_loop(0, groups, moved_chunk, 0)
        lax.fori_loop(0, groups, near_chunk, 0)

        def partial(k, piece, device):
            part = pl.ds(piece * piece_rows, piece_rows)
            return remote(
                part_out.at[k, part],
                part_in.at[step, k, part],
                part_send.at[0],
                part_recv.at[step, k, piece],
                device,
            )

        def gathered(k, chunk, part):
            return (
                near[chunk, part]
                + moved_in[step, 0, chunk, part].astype(jnp.float32)
                + moved_in[step, 1, chunk, part].astype(jnp.float32)
            )

        def await_moved(k, chunk):
            for d in range(2):

                @pl.when(has_source[d])
                def _():
                    to_sector(d, chunk, k).wait_recv()

        for k in range(groups - 1):
            chunk = order_of(k)
            device = ahead if k % 2 == 0 else behind
            await_moved(k, chunk)
            for piece in range(PIECES):
                part = pl.ds(piece * piece_rows, piece_rows)
                total = gathered(k, chunk, part)
                if k >= 2:
                    partial(k - 2, piece, device).wait_recv()
                    total += part_in[step, k - 2, part].astype(jnp.float32)
                part_out[k, part] = total.astype(part_out.dtype)
                partial(k, piece, device).start()

        await_moved(groups - 1, z)
        total = gathered(groups - 1, z, pl.ds(0, rows))
        for k in (groups - 3, groups - 2):
            for piece in range(PIECES):
                partial(k, piece, ahead).wait_recv()
            total += part_in[step, k].astype(jnp.float32)
        total = jnp.where(live, total, 0.0)

        for d in range(2):

            @pl.when(has_target[d])
            def _():
                remote(
                    moved_out.at[d], moved_out.at[d], moved_send.at[d], moved_send.at[d], partner
                ).wait_send()

        remote(part_out, part_out, part_send.at[0], part_send.at[0], partner).wait_send()
        sent = full.at[step, pl.ds(0, groups - 1), :, 0]
        remote(sent, sent, ring_send.at[step], ring_send.at[step], partner).wait_send()
        sent = full.at[step, :, :, 0]
        remote(sent, sent, cross_send.at[step], cross_send.at[step], partner).wait_send()

        @pl.when(step == 0)
        def _():
            full[1, z, :, h] = total.astype(full.dtype).reshape(bonds, half, cols)

        @pl.when(step == 1)
        def _():
            begin = full[0, z, :, h].reshape(rows, cols).astype(jnp.float32)
            last[...] = (2.0 * total - begin).astype(last.dtype).reshape(bonds, half, cols)

        return carry

    def send_back(out, block, slot):
        def one(i, carry):
            p = (me + i) % bonds
            remote(
                block.at[p], out.at[q, h], back_send.at[slot], back_recv.at[slot], (p, z)
            ).start()
            return carry

        lax.fori_loop(1, bonds, one, 0)
        pltpu.make_async_copy(block.at[me], out.at[q, h], local_sem.at[3 + slot]).start()

    def finish(out, block, slot):
        pltpu.make_async_copy(block.at[me], out.at[q, h], local_sem.at[3 + slot]).wait()
        remote(others, others, back_send.at[slot], back_recv.at[slot], partner).wait()

    lax.fori_loop(0, 2, apply, 0)
    send_back(second_out, last, 1)
    finish(first_out, full.at[1, z, :, h], 0)
    finish(second_out, last, 1)


def local(wavefunction, left_env, right_env, left_sizes, right_sizes, channel_shift):
    bonds = lax.axis_size("bond")
    groups = lax.axis_size("mpo")
    sectors, block_rows, states = wavefunction.shape
    half = block_rows // 2
    channels = left_env.shape[0]
    rows = bonds * half
    cols = states // groups
    out = jax.ShapeDtypeStruct((sectors, 2, half, cols), wavefunction.dtype)
    dtype = wavefunction.dtype
    dma = pltpu.SemaphoreType.DMA
    first, second = pl.pallas_call(
        kernel,
        out_shape=(out, out),
        in_specs=[pl.BlockSpec(memory_space=pl.ANY)] * 3
        + [pl.BlockSpec(memory_space=pltpu.SMEM)] * 3,
        out_specs=[pl.BlockSpec(memory_space=pl.ANY)] * 2,
        scratch_shapes=[
            pltpu.VMEM((channels, rows, states), dtype),
            pltpu.VMEM((channels, bonds, 2, half, states), dtype),
            pltpu.VMEM((bonds, half, cols), dtype),
            pltpu.VMEM((2, groups, bonds, 2, half, cols), dtype),
            pltpu.VMEM((channels, rows, states), dtype),
            pltpu.VMEM((groups, rows, cols), jnp.float32),
            pltpu.VMEM((2, groups, rows, cols), dtype),
            pltpu.VMEM((2, 2, groups, rows, cols), dtype),
            pltpu.VMEM((groups - 1, rows, cols), dtype),
            pltpu.VMEM((2, groups - 1, rows, cols), dtype),
            pltpu.VMEM((bonds, half, cols), dtype),
            dma((5,)),
            dma((2,)),
            dma((2,)),
            dma((2,)),
            dma((2, groups, PIECES)),
            dma((2,)),
            dma((2, groups, PIECES)),
            dma((2,)),
            dma((2, 2, groups)),
            dma((1,)),
            dma((2, groups - 1, PIECES)),
            dma((2,)),
            dma((2,)),
        ],
        compiler_params=pltpu.CompilerParams(
            collective_id=0, has_side_effects=True, vmem_limit_bytes=56 << 20
        ),
        cost_estimate=pl.CostEstimate(
            flops=8 * channels * rows * states * states,
            bytes_accessed=6 * channels * rows * states,
            transcendentals=0,
        ),
        name="two_steps",
    )(
        wavefunction,
        left_env.reshape(channels, rows, states),
        right_env.reshape(channels, bonds, half, states),
        left_sizes,
        right_sizes,
        channel_shift,
    )
    shape = (sectors, block_rows, cols)
    return first.reshape(shape), second.reshape(shape)


def solution(mesh):
    placed = (
        P(None, "bond", None),
        P("mpo", "bond", None, None),
        P("mpo", "bond", None, None),
        P(),
        P(),
        P(),
    )
    return jax.shard_map(
        local,
        mesh=mesh,
        in_specs=placed,
        out_specs=(P(None, "bond", "mpo"), P(None, "bond", "mpo")),
        check_vma=False,
    )
```

```python
import jax
import jax.numpy as jnp
from jax import lax
from jax.experimental import pallas as pl
from jax.experimental.pallas import tpu as pltpu
from jax.sharding import PartitionSpec as P

MESH = pl.DeviceIdType.MESH
PIECES = 2
Z_PART = 8
LAG = 1


def z_first_rows(rows):
    return rows * Z_PART // 32


def kernel(
    wave,
    left_env,
    right_env,
    left_sizes,
    right_sizes,
    channel_shift,
    first_out,
    second_out,
    left,
    right,
    start_in,
    full,
    mixed,
    near,
    moved_out,
    moved_in,
    y_part_out,
    y_part_in,
    z_part_out,
    z_part_in,
    late_out,
    late_in,
    last,
    local_sem,
    pair_sem,
    keep_sem,
    scatter_send,
    scatter_recv,
    ring_send,
    ring_recv,
    side_recv,
    cross_send,
    cross_recv,
    moved_send,
    moved_recv,
    part_send,
    y_part_recv,
    z_part_recv,
    late_send,
    late_recv,
    back_send,
    back_recv,
):
    bonds = lax.axis_size("bond")
    groups = lax.axis_size("mpo")
    me = lax.axis_index("bond")
    z = lax.axis_index("mpo")
    sectors = bonds // 2
    q = me // 2
    h = me % 2
    channels = left.shape[0]
    half = wave.shape[1] // 2
    rows = bonds * half
    cols = full.shape[-1]
    per_chunk = right.shape[1] // groups
    lines = bonds // PIECES
    y_rows = moved_in.shape[3]
    z_rows = rows - y_rows
    y_span = pl.ds(0, y_rows)
    z_span = pl.ds(y_rows, z_rows)
    turn = 1 - 2 * h
    partner = (me + turn, z)
    hops = groups // 2

    def chunk_at(offset):
        return (z + turn * offset + groups) % groups

    ahead = (me, chunk_at(1))
    behind = (me, chunk_at(-1))

    def remote(source, target, send, recv, device):
        return pltpu.make_async_remote_copy(
            src_ref=source,
            dst_ref=target,
            send_sem=send,
            recv_sem=recv,
            device_id=device,
            device_id_type=MESH,
        )

    def await_sent(block, sem):
        remote(block, block, sem, sem, partner).wait_send()

    right_own = right.at[:, :, h]
    load_left = pltpu.make_async_copy(left_env, left, local_sem.at[0])
    load_right = pltpu.make_async_copy(right_env, right_own, local_sem.at[1])
    swap_right = remote(right_env, right_own, pair_sem.at[0], pair_sem.at[1], partner)
    load_left.start()
    load_right.start()

    barrier = pltpu.get_barrier_semaphore()

    def greet(i, carry):
        pl.semaphore_signal(
            barrier, inc=1, device_id=((me + i) % bonds, z), device_id_type=MESH
        )
        return carry

    pl.semaphore_signal(barrier, inc=1, device_id=ahead, device_id_type=MESH)
    pl.semaphore_signal(barrier, inc=1, device_id=behind, device_id_type=MESH)
    lax.fori_loop(1, bonds, greet, 0)
    pl.semaphore_wait(barrier, bonds + 1)

    swap_right.start()

    def piece_of_wave(p, chunk):
        return wave.at[
            p // 2,
            pl.ds(pl.multiple_of((p % 2) * half, half), half),
            pl.ds(pl.multiple_of(chunk * cols, cols), cols),
        ]

    ours = [z % 2 + 2 * j for j in range(hops)]
    theirs = [1 - z % 2 + 2 * j for j in range(hops)]

    def scatter(j, i):
        p = (me + i) % bonds
        remote(
            piece_of_wave(p, ours[j]),
            start_in.at[j, me],
            scatter_send.at[0],
            scatter_recv.at[j],
            (p, z),
        ).start()

    def keep(j):
        return pltpu.make_async_copy(piece_of_wave(me, ours[j]), start_in.at[j, me], keep_sem.at[j])

    for j in range(hops):

        def spread(i, carry, j=j):
            scatter(j, i)
            return carry

        keep(j).start()
        lax.fori_loop(1, bonds, spread, 0)

    for step in range(2):
        for d, outside in ((0, 0), (1, sectors - 1)):

            @pl.when(q == outside)
            def _():
                moved_in[step, d] = jnp.zeros(moved_in.shape[2:], moved_in.dtype)
                late_in[step, d] = jnp.zeros(late_in.shape[2:], late_in.dtype)

        for k in range(2):
            y_part_in[step, k] = jnp.zeros(y_part_in.shape[2:], y_part_in.dtype)
            z_part_in[step, k] = jnp.zeros(z_part_in.shape[2:], z_part_in.dtype)

    def live(first, count, chunk=z):
        row = lax.broadcasted_iota(jnp.int32, (count, cols), 0) + first
        col = lax.broadcasted_iota(jnp.int32, (count, cols), 1)
        row = (row // half) * (2 * half) + h * half + row % half
        return (row < left_sizes[q]) & (col + chunk * cols < right_sizes[q])

    def channel_of(shift):
        found = channels - 1
        for j in range(channels - 1):
            found = jnp.where(channel_shift[z * channels + j] == shift, j, found)
        return found

    order = [channel_of(1), channel_of(-1), channel_of(0)]

    def apply(step, carry):
        def line_set(chunk, piece):
            return full.at[step, chunk, pl.ds(piece * lines, lines), h]

        def pass_on(chunk, slot, piece, device):
            block = line_set(chunk, piece)
            return remote(block, block, ring_send.at[0], ring_recv.at[slot, piece], device)

        def share(chunk, piece):
            block = line_set(chunk, piece)
            return remote(
                block, block, cross_send.at[0], cross_recv.at[step, chunk, piece], partner
            )

        def mix_units(chunks):
            def unit(d):
                if d == 0:
                    for chunk in chunks:
                        for piece in range(PIECES):
                            share(chunk, piece).wait_recv()
                sets = [chunks]
                for some in sets:
                    vector = [full[step, chunk].reshape(2 * rows, cols) for chunk in some]
                    vector = vector[0] if len(vector) == 1 else jnp.concatenate(vector, axis=1)
                    block = jnp.dot(
                        left[order[d]], vector, preferred_element_type=jnp.float32
                    ).astype(mixed.dtype)
                    for n, chunk in enumerate(some):
                        mixed[d, :, pl.ds(pl.multiple_of(chunk * cols, cols), cols)] = block[
                            :, n * cols : (n + 1) * cols
                        ]

            return [lambda d=d: unit(d) for d in range(channels)]

        def run(queue, count=channels):
            for unit in queue[:count]:
                unit()
            del queue[:count]

        def to_side(j, chunk, way):
            block = full.at[0, chunk, :, h]
            return remote(
                block, block, ring_send.at[0], side_recv.at[j], (me, (z + way + groups) % groups)
            )

        @pl.when(step == 0)
        def _():
            def begin(j):
                keep(j).wait()
                others = start_in.at[j, pl.ds(0, bonds - 1)]
                remote(others, others, scatter_send.at[0], scatter_recv.at[j], partner).wait_recv()
                block = start_in[j].reshape(rows, cols)
                block = jnp.where(live(0, rows, ours[j]), block, jnp.zeros((), block.dtype))
                full[0, ours[j], :, h] = block.reshape(bonds, half, cols)
                to_side(j, ours[j], 1 - 2 * (j % 2)).start()
                for piece in range(PIECES):
                    share(ours[j], piece).start()

            def arrive(j):
                to_side(j, theirs[j], 1).wait_recv()
                for piece in range(PIECES):
                    share(theirs[j], piece).start()

            begin(0)
            begin(1)
            load_left.wait()
            queue = mix_units(ours[:2])
            for j in range(2, hops):
                begin(j)
                run(queue, 1)
            run(queue)
            queue = mix_units(ours[2:]) if hops > 2 else []
            for j in range(hops):
                arrive(j)
                run(queue, 1 + j % 2)
                if j % 2:
                    queue += mix_units(theirs[j - 1 : j + 1])
            run(queue, len(queue))
            sent = start_in.at[:, pl.ds(0, bonds - 1)]
            await_sent(sent, scatter_send.at[0])
            await_sent(full.at[0, pl.ds(0, hops), :, 0], ring_send.at[0])
            load_right.wait()
            swap_right.wait()

        @pl.when(step == 1)
        def _():
            for piece in range(PIECES):
                pass_on(z, 0, piece, ahead).start()
                pass_on(z, 1, piece, behind).start()
            for piece in range(PIECES):
                share(z, piece).start()
            send_back(first_out, full.at[1, z, :, h], 0)
            queue = mix_units([z])
            run(queue)
            for s in range(1, hops + 1):
                from_behind, from_ahead = chunk_at(-s), chunk_at(s)
                for piece in range(PIECES):
                    pass_on(from_behind, 2 * s - 2, piece, ahead).wait_recv()
                    if s < hops:
                        pass_on(from_behind, 2 * s, piece, ahead).start()
                    share(from_behind, piece).start()
                    if s < hops:
                        pass_on(from_ahead, 2 * s - 1, piece, behind).wait_recv()
                        if s < hops - 1:
                            pass_on(from_ahead, 2 * s + 1, piece, behind).start()
                        share(from_ahead, piece).start()
                    run(queue, 2 - piece)
                run(queue)
                queue = mix_units([from_behind, from_ahead] if s < hops else [from_behind])
            run(queue)
            await_sent(full.at[1, pl.ds(0, groups - 1), :, 0], ring_send.at[0])

        def order_of(k):
            distance = hops - (k + 1) // 2
            return chunk_at(distance * (1 - 2 * (k % 2)))

        def images(d, pair):
            blocks = [
                right[order[d], pl.ds(chunk * per_chunk, per_chunk)].reshape(cols, -1)
                for chunk in pair
            ]
            both = lax.dot_general(
                mixed[d],
                jnp.concatenate(blocks, axis=0),
                (((1,), (1,)), ((), ())),
                preferred_element_type=jnp.float32,
            )
            return both[:, :cols], both[:, cols:]

        has_target = [(q < sectors - 1), (q > 0)]
        has_source = [(q > 0), (q < sectors - 1)]

        def to_sector(d, chunk, k, device=partner):
            return remote(
                moved_out.at[d, chunk, y_span],
                moved_in.at[step, d, chunk],
                moved_send.at[d],
                moved_recv.at[step, d, k],
                device,
            )

        def late(d, device=partner):
            return remote(
                late_out.at[d], late_in.at[step, d], late_send.at[d], late_recv.at[step, d], device
            )

        def neighbour(d):
            return (me + (2 if d == 0 else -2), z)

        def way_of(k):
            return (me, chunk_at(1 - 2 * (k % 2)))

        def z_partial(k, device=partner):
            return remote(
                z_part_out.at[k],
                z_part_in.at[step, k + 2],
                part_send.at[0],
                z_part_recv.at[step, k],
                device,
            )

        def y_part(piece):
            return pl.ds(piece * (y_rows // PIECES), y_rows // PIECES)

        def y_partial(k, piece, device=partner):
            return remote(
                y_part_out.at[k, y_part(piece)],
                y_part_in.at[step, k + 2, y_part(piece)],
                part_send.at[1],
                y_part_recv.at[step, k, piece],
                device,
            )

        def z_terms(chunk):
            return [
                near[chunk, z_span],
                moved_out[0, chunk, z_span].astype(jnp.float32),
                moved_out[1, chunk, z_span].astype(jnp.float32),
            ]

        def y_terms(chunk, part=y_span):
            return (
                near[chunk, part]
                + moved_in[step, 0, chunk, part].astype(jnp.float32)
                + moved_in[step, 1, chunk, part].astype(jnp.float32)
            )

        def await_moved(k, chunk):
            for d in range(2):

                @pl.when(has_source[d])
                def _():
                    to_sector(d, chunk, k).wait_recv()

        def z_hop(k):
            chunk = order_of(k)

            @pl.when((k >= 2))
            def _():
                z_partial(k - 2).wait_recv()

            for i, term in enumerate(z_terms(chunk)):
                term += z_part_in[step, k, i].astype(jnp.float32)
                z_part_out[k, i] = term.astype(z_part_out.dtype)
            z_partial(k, way_of(k)).start()

        def y_hop(k):
            chunk = order_of(k)
            await_moved(k, chunk)
            for piece in range(PIECES):
                part = y_part(piece)

                @pl.when((k >= 2))
                def _():
                    y_partial(k - 2, piece).wait_recv()

                total = y_terms(chunk, part) + y_part_in[step, k, part].astype(jnp.float32)
                y_part_out[k, part] = total.astype(y_part_out.dtype)
                y_partial(k, piece, way_of(k)).start()

        def round_of_ring(t, inner):
            @pl.when(t < hops)
            def _():
                pair = (order_of(2 * t), order_of(2 * t + 1))
                for d in range(2):
                    blocks = images(d, pair)
                    for n, chunk in enumerate(pair):
                        moved_out[d, chunk] = blocks[n].astype(moved_out.dtype)

                        @pl.when(has_target[d])
                        def _():
                            to_sector(d, chunk, 2 * t + n, neighbour(d)).start()

                near[pair[0]], near[pair[1]] = images(2, pair)

            for hop, lag in ((z_hop, 1), (y_hop, LAG)):

                @pl.when((t >= lag) & (t < lag + hops))
                def _():
                    hop(2 * (t - lag))

                @pl.when((t >= lag) & (t < lag + hops - 1))
                def _():
                    hop(2 * (t - lag) + 1)

            return inner

        lax.fori_loop(0, hops + LAG, round_of_ring, 0)

        z_total = z_terms(z)
        for k in (groups - 3, groups - 2):
            z_partial(k).wait_recv()
            for i in range(3):
                z_total[i] += z_part_in[step, k + 2, i].astype(jnp.float32)
        for d in range(2):
            late_out[d] = z_total[1 + d].astype(late_out.dtype)

            @pl.when(has_target[d])
            def _():
                late(d, neighbour(d)).start()

        await_moved(groups - 1, z)
        total = y_terms(z)
        for k in (groups - 3, groups - 2):
            for piece in range(PIECES):
                y_partial(k, piece).wait_recv()
            total += y_part_in[step, k + 2].astype(jnp.float32)

        def conclude(value, first, count):
            value = jnp.where(live(first, count), value, 0.0)
            span = pl.ds(first // half, count // half)
            shape = (count // half, half, cols)

            @pl.when(step == 0)
            def _():
                full[1, z, span, h] = value.astype(full.dtype).reshape(shape)

            @pl.when(step == 1)
            def _():
                begin = full[0, z, span, h].reshape(count, cols).astype(jnp.float32)
                last[span] = (2.0 * value - begin).astype(last.dtype).reshape(shape)

        conclude(total, 0, y_rows)
        for d in range(2):

            @pl.when(has_source[d])
            def _():
                late(d).wait_recv()

        total = (
            z_total[0]
            + late_in[step, 0].astype(jnp.float32)
            + late_in[step, 1].astype(jnp.float32)
        )
        conclude(total, y_rows, z_rows)

        for d in range(2):

            @pl.when(has_target[d])
            def _():
                await_sent(moved_out.at[d, :, y_span], moved_send.at[d])
                late(d).wait_send()

        await_sent(z_part_out, part_send.at[0])
        await_sent(y_part_out, part_send.at[1])
        await_sent(full.at[step, :, :, 0], cross_send.at[0])
        return carry

    def send_back(out, block, slot):
        def one(i, carry):
            p = (me + i) % bonds
            remote(
                block.at[p], out.at[q, h], back_send.at[slot], back_recv.at[slot], (p, z)
            ).start()
            return carry

        lax.fori_loop(1, bonds, one, 0)
        pltpu.make_async_copy(block.at[me], out.at[q, h], local_sem.at[2 + slot]).start()

    def finish(out, block, slot):
        pltpu.make_async_copy(block.at[me], out.at[q, h], local_sem.at[2 + slot]).wait()
        others = start_in.at[0, pl.ds(0, bonds - 1)]
        remote(others, others, back_send.at[slot], back_recv.at[slot], partner).wait()

    lax.fori_loop(0, 2, apply, 0)
    send_back(second_out, last, 1)
    finish(first_out, full.at[1, z, :, h], 0)
    finish(second_out, last, 1)


def local(wavefunction, left_env, right_env, left_sizes, right_sizes, channel_shift):
    bonds = lax.axis_size("bond")
    groups = lax.axis_size("mpo")
    sectors, block_rows, states = wavefunction.shape
    half = block_rows // 2
    channels = left_env.shape[0]
    rows = bonds * half
    cols = states // groups
    z_rows = z_first_rows(rows)
    y_rows = rows - z_rows
    dtype = wavefunction.dtype
    out = jax.ShapeDtypeStruct((sectors, 2, half, cols), dtype)
    dma = pltpu.SemaphoreType.DMA
    first, second = pl.pallas_call(
        kernel,
        out_shape=(out, out),
        in_specs=[pl.BlockSpec(memory_space=pl.ANY)] * 3
        + [pl.BlockSpec(memory_space=pltpu.SMEM)] * 3,
        out_specs=[pl.BlockSpec(memory_space=pl.ANY)] * 2,
        scratch_shapes=[
            pltpu.VMEM((channels, rows, states), dtype),
            pltpu.VMEM((channels, bonds, 2, half, states), dtype),
            pltpu.VMEM((groups // 2, bonds, half, cols), dtype),
            pltpu.VMEM((2, groups, bonds, 2, half, cols), dtype),
            pltpu.VMEM((channels, rows, states), dtype),
            pltpu.VMEM((groups, rows, cols), jnp.float32),
            pltpu.VMEM((2, groups, rows, cols), dtype),
            pltpu.VMEM((2, 2, groups, y_rows, cols), dtype),
            pltpu.VMEM((groups - 1, y_rows, cols), dtype),
            pltpu.VMEM((2, groups + 1, y_rows, cols), dtype),
            pltpu.VMEM((groups - 1, 3, z_rows, cols), dtype),
            pltpu.VMEM((2, groups + 1, 3, z_rows, cols), dtype),
            pltpu.VMEM((2, z_rows, cols), dtype),
            pltpu.VMEM((2, 2, z_rows, cols), dtype),
            pltpu.VMEM((bonds, half, cols), dtype),
            dma((4,)),
            dma((2,)),
            dma((groups // 2,)),
            dma((1,)),
            dma((groups // 2,)),
            dma((1,)),
            dma((groups - 1, PIECES)),
            dma((groups // 2,)),
            dma((1,)),
            dma((2, groups, PIECES)),
            dma((2,)),
            dma((2, 2, groups)),
            dma((2,)),
            dma((2, groups - 1, PIECES)),
            dma((2, groups - 1)),
            dma((2,)),
            dma((2, 2)),
            dma((2,)),
            dma((2,)),
        ],
        compiler_params=pltpu.CompilerParams(
            collective_id=0, has_side_effects=True, vmem_limit_bytes=56 << 20
        ),
        cost_estimate=pl.CostEstimate(
            flops=8 * channels * rows * states * states,
            bytes_accessed=6 * channels * rows * states,
            transcendentals=0,
        ),
        name="two_steps",
    )(
        wavefunction,
        left_env.reshape(channels, rows, states),
        right_env.reshape(channels, bonds, half, states),
        left_sizes,
        right_sizes,
        channel_shift,
    )
    shape = (sectors, block_rows, cols)
    return first.reshape(shape), second.reshape(shape)


def solution(mesh):
    placed = (
        P(None, "bond", None),
        P("mpo", "bond", None, None),
        P("mpo", "bond", None, None),
        P(),
        P(),
        P(),
    )
    return jax.shard_map(
        local,
        mesh=mesh,
        in_specs=placed,
        out_specs=(P(None, "bond", "mpo"), P(None, "bond", "mpo")),
        check_vma=False,
    )
```

```python
import jax
import jax.numpy as jnp
from jax import lax
from jax.experimental import pallas as pl
from jax.experimental.pallas import tpu as pltpu
from jax.sharding import PartitionSpec as P

MESH = pl.DeviceIdType.MESH
PIECES = 2
REACH = 2


def kernel(
    wave,
    left_env,
    right_env,
    left_sizes,
    right_sizes,
    channel_shift,
    first_out,
    second_out,
    left,
    right,
    start_in,
    full,
    mixed,
    near,
    moved_out,
    moved_in,
    part_out,
    part_in,
    near_out,
    beside_in,
    late_out,
    late_in,
    last,
    local_sem,
    pair_sem,
    keep_sem,
    scatter_send,
    scatter_recv,
    ring_send,
    ring_recv,
    side_recv,
    cross_send,
    cross_recv,
    moved_send,
    moved_recv,
    part_send,
    part_recv,
    beside_send,
    beside_recv,
    late_send,
    late_recv,
    back_send,
    back_recv,
):
    bonds = lax.axis_size("bond")
    groups = lax.axis_size("mpo")
    me = lax.axis_index("bond")
    z = lax.axis_index("mpo")
    sectors = bonds // 2
    q = me // 2
    h = me % 2
    channels = left.shape[0]
    half = wave.shape[1] // 2
    rows = bonds * half
    cols = full.shape[-1]
    per_chunk = right.shape[1] // groups
    lines = bonds // PIECES
    turn = 1 - 2 * h
    partner = (me + turn, z)
    hops = groups // 2

    def chunk_at(offset):
        return (z + turn * offset + groups) % groups

    ahead = (me, chunk_at(1))
    behind = (me, chunk_at(-1))

    def parent(o):
        return 0 if abs(o) <= REACH else (REACH if o > 0 else -REACH)

    offsets = range(1 - hops, hops + 1)

    def children(o):
        return [c for c in offsets if abs(c) > 1 and parent(c) == o]

    far = [o for o in offsets if abs(o) > 1]
    pairs = [(hops, hops - 1), (1, -1), (1 - hops, 2), (-2, 0)]
    if hops == 2:
        pairs = [(2, 1), (-1, 0)]

    def remote(source, target, send, recv, device):
        return pltpu.make_async_remote_copy(
            src_ref=source,
            dst_ref=target,
            send_sem=send,
            recv_sem=recv,
            device_id=device,
            device_id_type=MESH,
        )

    def await_sent(block, sem):
        remote(block, block, sem, sem, partner).wait_send()

    right_own = right.at[:, :, h]
    load_left = pltpu.make_async_copy(left_env, left, local_sem.at[0])
    load_right = pltpu.make_async_copy(right_env, right_own, local_sem.at[1])
    swap_right = remote(right_env, right_own, pair_sem.at[0], pair_sem.at[1], partner)
    load_left.start()
    load_right.start()

    barrier = pltpu.get_barrier_semaphore()

    def greet(i, carry):
        pl.semaphore_signal(
            barrier, inc=1, device_id=((me + i) % bonds, z), device_id_type=MESH
        )
        return carry

    for distance in range(1, REACH + 1):
        for way in (distance, -distance):
            pl.semaphore_signal(
                barrier, inc=1, device_id=(me, chunk_at(way)), device_id_type=MESH
            )
    lax.fori_loop(1, bonds, greet, 0)
    pl.semaphore_wait(barrier, bonds - 1 + 2 * REACH)

    swap_right.start()

    def piece_of_wave(p, chunk):
        return wave.at[
            p // 2,
            pl.ds(pl.multiple_of((p % 2) * half, half), half),
            pl.ds(pl.multiple_of(chunk * cols, cols), cols),
        ]

    ours = [z % 2 + 2 * j for j in range(hops)]
    theirs = [1 - z % 2 + 2 * j for j in range(hops)]

    def scatter(j, i):
        p = (me + i) % bonds
        remote(
            piece_of_wave(p, ours[j]),
            start_in.at[j, me],
            scatter_send.at[0],
            scatter_recv.at[j],
            (p, z),
        ).start()

    def keep(j):
        return pltpu.make_async_copy(piece_of_wave(me, ours[j]), start_in.at[j, me], keep_sem.at[j])

    for j in range(hops):

        def spread(i, carry, j=j):
            scatter(j, i)
            return carry

        keep(j).start()
        lax.fori_loop(1, bonds, spread, 0)

    for step in range(2):
        for d, outside in ((0, 0), (1, sectors - 1)):

            @pl.when(q == outside)
            def _():
                moved_in[step, d] = jnp.zeros(moved_in.shape[2:], moved_in.dtype)
                late_in[step, d] = jnp.zeros(late_in.shape[2:], late_in.dtype)

    def live(first, count, chunk=z):
        row = lax.broadcasted_iota(jnp.int32, (count, cols), 0) + first
        col = lax.broadcasted_iota(jnp.int32, (count, cols), 1)
        row = (row // half) * (2 * half) + h * half + row % half
        return (row < left_sizes[q]) & (col + chunk * cols < right_sizes[q])

    def channel_of(shift):
        found = channels - 1
        for j in range(channels - 1):
            found = jnp.where(channel_shift[z * channels + j] == shift, j, found)
        return found

    order = [channel_of(1), channel_of(-1), channel_of(0)]

    def apply(step, carry):
        def line_set(chunk, piece):
            return full.at[step, chunk, pl.ds(piece * lines, lines), h]

        def pass_on(chunk, slot, piece, device):
            block = line_set(chunk, piece)
            return remote(block, block, ring_send.at[0], ring_recv.at[slot, piece], device)

        def share(chunk, piece):
            block = line_set(chunk, piece)
            return remote(
                block, block, cross_send.at[0], cross_recv.at[step, chunk, piece], partner
            )

        def mix_units(chunks):
            def unit(d):
                if d == 0:
                    for chunk in chunks:
                        for piece in range(PIECES):
                            share(chunk, piece).wait_recv()
                sets = [chunks]
                for some in sets:
                    vector = [full[step, chunk].reshape(2 * rows, cols) for chunk in some]
                    vector = vector[0] if len(vector) == 1 else jnp.concatenate(vector, axis=1)
                    block = jnp.dot(
                        left[order[d]], vector, preferred_element_type=jnp.float32
                    ).astype(mixed.dtype)
                    for n, chunk in enumerate(some):
                        mixed[d, :, pl.ds(pl.multiple_of(chunk * cols, cols), cols)] = block[
                            :, n * cols : (n + 1) * cols
                        ]

            return [lambda d=d: unit(d) for d in range(channels)]

        def run(queue, count=channels):
            for unit in queue[:count]:
                unit()
            del queue[:count]

        def to_side(j, chunk, way):
            block = full.at[0, chunk, :, h]
            return remote(
                block, block, ring_send.at[0], side_recv.at[j], (me, (z + way + groups) % groups)
            )

        @pl.when(step == 0)
        def _():
            def begin(j):
                keep(j).wait()
                others = start_in.at[j, pl.ds(0, bonds - 1)]
                remote(others, others, scatter_send.at[0], scatter_recv.at[j], partner).wait_recv()
                block = start_in[j].reshape(rows, cols)
                block = jnp.where(live(0, rows, ours[j]), block, jnp.zeros((), block.dtype))
                full[0, ours[j], :, h] = block.reshape(bonds, half, cols)
                to_side(j, ours[j], 1 - 2 * (j % 2)).start()
                for piece in range(PIECES):
                    share(ours[j], piece).start()

            def arrive(j):
                to_side(j, theirs[j], 1).wait_recv()
                for piece in range(PIECES):
                    share(theirs[j], piece).start()

            begin(0)
            begin(1)
            load_left.wait()
            queue = mix_units(ours[:2])
            for j in range(2, hops):
                begin(j)
                run(queue, 1)
            run(queue)
            queue = mix_units(ours[2:]) if hops > 2 else []
            for j in range(hops):
                arrive(j)
                run(queue, 1 + j % 2)
                if j % 2:
                    queue += mix_units(theirs[j - 1 : j + 1])
            run(queue, len(queue))
            sent = start_in.at[:, pl.ds(0, bonds - 1)]
            await_sent(sent, scatter_send.at[0])
            await_sent(full.at[0, pl.ds(0, hops), :, 0], ring_send.at[0])
            load_right.wait()
            swap_right.wait()

        @pl.when(step == 1)
        def _():
            for piece in range(PIECES):
                pass_on(z, 0, piece, ahead).start()
                pass_on(z, 1, piece, behind).start()
            for piece in range(PIECES):
                share(z, piece).start()
            queue = mix_units([z])
            run(queue)
            for s in range(1, hops + 1):
                from_behind, from_ahead = chunk_at(-s), chunk_at(s)
                for piece in range(PIECES):
                    pass_on(from_behind, 2 * s - 2, piece, ahead).wait_recv()
                    if s < hops:
                        pass_on(from_behind, 2 * s, piece, ahead).start()
                    share(from_behind, piece).start()
                    if s < hops:
                        pass_on(from_ahead, 2 * s - 1, piece, behind).wait_recv()
                        if s < hops - 1:
                            pass_on(from_ahead, 2 * s + 1, piece, behind).start()
                        share(from_ahead, piece).start()
                    run(queue, 2 - piece)
                run(queue)
                queue = mix_units([from_behind, from_ahead] if s < hops else [from_behind])
            run(queue)
            await_sent(full.at[1, pl.ds(0, groups - 1), :, 0], ring_send.at[0])

        def images(d, pair):
            blocks = [
                right[order[d], pl.ds(chunk * per_chunk, per_chunk)].reshape(cols, -1)
                for chunk in pair
            ]
            both = lax.dot_general(
                mixed[d],
                jnp.concatenate(blocks, axis=0),
                (((1,), (1,)), ((), ())),
                preferred_element_type=jnp.float32,
            )
            return both[:, :cols], both[:, cols:]

        has_target = [(q < sectors - 1), (q > 0)]
        has_source = [(q > 0), (q < sectors - 1)]

        def to_sector(d, o, device=partner):
            chunk = chunk_at(o)
            return remote(
                moved_out.at[d, chunk],
                moved_in.at[step, d, chunk],
                moved_send.at[d, o + hops - 1],
                moved_recv.at[step, d, o + hops - 1],
                device,
            )

        def late(d, device=partner):
            return remote(
                late_out.at[d], late_in.at[step, d], late_send.at[d], late_recv.at[step, d], device
            )

        def neighbour(d):
            return (me + (2 if d == 0 else -2), z)

        def to_beside(o, i):
            side = (1 - o) // 2
            source = moved_out.at[i, chunk_at(o)] if i < 2 else near_out.at[side]
            return remote(
                source,
                beside_in.at[step, side, i],
                beside_send.at[i // 2],
                beside_recv.at[step, side, i],
                (me, chunk_at(o)),
            )

        def partial(o):
            slot = o + hops - 1
            return remote(
                part_out.at[slot],
                part_in.at[step, slot],
                part_send.at[0],
                part_recv.at[step, slot],
                (me, chunk_at(o - parent(o))),
            )

        def add_children(o, total):
            for c in children(o):
                partial(c).wait_recv()
                total += part_in[step, c + hops - 1].astype(jnp.float32)
            return total

        def hop(o):
            chunk = chunk_at(o)
            total = near[chunk]
            for d in range(2):

                @pl.when(has_source[d])
                def _():
                    to_sector(d, o).wait_recv()

                total += moved_in[step, d, chunk].astype(jnp.float32)
            part_out[o + hops - 1] = add_children(o, total).astype(part_out.dtype)
            partial(o).start()

        def image_pair(u, inner):
            first, second = pairs[-1]
            for t in range(len(pairs) - 1):
                first = jnp.where(u == t, pairs[t][0], first)
                second = jnp.where(u == t, pairs[t][1], second)
            pair = (chunk_at(first), chunk_at(second))
            for d in range(2):
                blocks = images(d, pair)
                for n, chunk in enumerate(pair):
                    moved_out[d, chunk] = blocks[n].astype(moved_out.dtype)
                for t, some in enumerate(pairs):
                    for o in some:

                        if o > REACH or hops == 2 and o == 2:

                            @pl.when((u == t) & has_target[d])
                            def _():
                                to_sector(d, o, neighbour(d)).start()

                        if abs(o) == 1:

                            @pl.when((u == t))
                            def _():
                                to_beside(o, d).start()

            near[pair[0]], near[pair[1]] = images(2, pair)
            return inner

        lax.fori_loop(0, len(pairs), image_pair, 0)

        @pl.when(step == 1)
        def _():
            send_back(first_out, full.at[1, z, :, h], 0)

        def send_after(o, done):
            for d in range(2):

                @pl.when(has_target[d])
                def _():
                    to_sector(d, done).wait_send()
                    if o:
                        to_sector(d, o, neighbour(d)).start()
                    else:
                        late(d, neighbour(d)).start()

        def merge_own():
            for d in range(2):
                moved = moved_out[d, z].astype(jnp.float32)
                for o in (1, -1):
                    to_beside(o, d).wait_recv()
                    moved += beside_in[step, (1 - o) // 2, d].astype(jnp.float32)
                late_out[d] = moved.astype(late_out.dtype)

        def send_beside():
            for o in (1, -1):
                near_out[(1 - o) // 2] = near[chunk_at(o)].astype(near_out.dtype)
                to_beside(o, 2).start()

        if hops == 2:
            send_beside()
            merge_own()
            send_after(0, 2)
            hop(2)
        else:
            send_after(-3, 4)
            hop(4)
            send_after(2, 3)
            hop(3)
            send_beside()
            send_after(-2, -3)
            hop(-3)
            merge_own()
            send_after(0, 2)
            hop(2)
            hop(-2)
            for d in range(2):

                @pl.when(has_target[d])
                def _():
                    to_sector(d, -2).wait_send()

        total = near[z]
        for o in (1, -1):
            to_beside(o, 2).wait_recv()
            total += beside_in[step, (1 - o) // 2, 2].astype(jnp.float32)
        total = add_children(0, total)
        for d in range(2):

            @pl.when(has_source[d])
            def _():
                late(d).wait_recv()

            total += late_in[step, d].astype(jnp.float32)

        def conclude(value, first, count):
            value = jnp.where(live(first, count), value, 0.0)
            span = pl.ds(first // half, count // half)
            shape = (count // half, half, cols)

            @pl.when(step == 0)
            def _():
                full[1, z, span, h] = value.astype(full.dtype).reshape(shape)

            @pl.when(step == 1)
            def _():
                begin = full[0, z, span, h].reshape(count, cols).astype(jnp.float32)
                last[span] = (2.0 * value - begin).astype(last.dtype).reshape(shape)

        conclude(total, 0, rows)

        for d in range(2):

            @pl.when(has_target[d])
            def _():
                late(d).wait_send()

        await_sent(moved_out.at[0, pl.ds(0, 4)], beside_send.at[0])
        await_sent(near_out, beside_send.at[1])
        await_sent(part_out.at[pl.ds(0, len(far))], part_send.at[0])
        await_sent(full.at[step, :, :, 0], cross_send.at[0])
        return carry

    def send_back(out, block, slot):
        def one(i, carry):
            p = (me + i) % bonds
            remote(
                block.at[p], out.at[q, h], back_send.at[slot], back_recv.at[slot], (p, z)
            ).start()
            return carry

        lax.fori_loop(1, bonds, one, 0)
        pltpu.make_async_copy(block.at[me], out.at[q, h], local_sem.at[2 + slot]).start()

    def finish(out, block, slot):
        pltpu.make_async_copy(block.at[me], out.at[q, h], local_sem.at[2 + slot]).wait()
        others = start_in.at[0, pl.ds(0, bonds - 1)]
        remote(others, others, back_send.at[slot], back_recv.at[slot], partner).wait()

    lax.fori_loop(0, 2, apply, 0)
    send_back(second_out, last, 1)
    finish(first_out, full.at[1, z, :, h], 0)
    finish(second_out, last, 1)


def hand_over(first, second, first_out, second_out):
    first_out[...] = first[...]
    second_out[...] = second[...]


def local(wavefunction, left_env, right_env, left_sizes, right_sizes, channel_shift):
    bonds = lax.axis_size("bond")
    groups = lax.axis_size("mpo")
    sectors, block_rows, states = wavefunction.shape
    half = block_rows // 2
    channels = left_env.shape[0]
    rows = bonds * half
    cols = states // groups
    dtype = wavefunction.dtype
    out = jax.ShapeDtypeStruct((sectors, 2, half, cols), dtype)
    dma = pltpu.SemaphoreType.DMA
    first, second = pl.pallas_call(
        kernel,
        out_shape=(out, out),
        in_specs=[pl.BlockSpec(memory_space=pl.ANY)] * 3
        + [pl.BlockSpec(memory_space=pltpu.SMEM)] * 3,
        out_specs=[pl.BlockSpec(memory_space=pl.ANY)] * 2,
        scratch_shapes=[
            pltpu.VMEM((channels, rows, states), dtype),
            pltpu.VMEM((channels, bonds, 2, half, states), dtype),
            pltpu.VMEM((groups // 2, bonds, half, cols), dtype),
            pltpu.VMEM((2, groups, bonds, 2, half, cols), dtype),
            pltpu.VMEM((channels, rows, states), dtype),
            pltpu.VMEM((groups, rows, cols), jnp.float32),
            pltpu.VMEM((2, groups, rows, cols), dtype),
            pltpu.VMEM((2, 2, groups, rows, cols), dtype),
            pltpu.VMEM((groups, rows, cols), dtype),
            pltpu.VMEM((2, groups, rows, cols), dtype),
            pltpu.VMEM((2, rows, cols), dtype),
            pltpu.VMEM((2, 2, 3, rows, cols), dtype),
            pltpu.VMEM((2, rows, cols), dtype),
            pltpu.VMEM((2, 2, rows, cols), dtype),
            pltpu.VMEM((bonds, half, cols), dtype),
            dma((4,)),
            dma((2,)),
            dma((groups // 2,)),
            dma((1,)),
            dma((groups // 2,)),
            dma((1,)),
            dma((groups - 1, PIECES)),
            dma((groups // 2,)),
            dma((1,)),
            dma((2, groups, PIECES)),
            dma((2, groups)),
            dma((2, 2, groups)),
            dma((1,)),
            dma((2, groups)),
            dma((2,)),
            dma((2, 2, 3)),
            dma((2,)),
            dma((2, 2)),
            dma((2,)),
            dma((2,)),
        ],
        compiler_params=pltpu.CompilerParams(
            collective_id=0, has_side_effects=True, vmem_limit_bytes=56 << 20
        ),
        cost_estimate=pl.CostEstimate(
            flops=8 * channels * rows * states * states,
            bytes_accessed=6 * channels * rows * states,
            transcendentals=0,
        ),
        name="two_steps",
    )(
        wavefunction,
        left_env.reshape(channels, rows, states),
        right_env.reshape(channels, bonds, half, states),
        left_sizes,
        right_sizes,
        channel_shift,
    )
    first, second = pl.pallas_call(hand_over, out_shape=(out, out), name="hand_over")(
        first, second
    )
    shape = (sectors, block_rows, cols)
    return first.reshape(shape), second.reshape(shape)


def solution(mesh):
    placed = (
        P(None, "bond", None),
        P("mpo", "bond", None, None),
        P("mpo", "bond", None, None),
        P(),
        P(),
        P(),
    )
    return jax.shard_map(
        local,
        mesh=mesh,
        in_specs=placed,
        out_specs=(P(None, "bond", "mpo"), P(None, "bond", "mpo")),
        check_vma=False,
    )
```

```python
import jax
import jax.numpy as jnp
from jax import lax
from jax.experimental import pallas as pl
from jax.experimental.pallas import tpu as pltpu
from jax.sharding import PartitionSpec as P

MESH = pl.DeviceIdType.MESH
PIECES = 2
REACH = 2


def kernel(
    wave,
    left_env,
    right_env,
    left_sizes,
    right_sizes,
    channel_shift,
    first_out,
    second_out,
    left,
    right,
    start_in,
    full,
    mixed,
    near,
    moved_out,
    moved_in,
    part_out,
    part_in,
    near_out,
    beside_in,
    late_out,
    late_in,
    last,
    local_sem,
    pair_sem,
    keep_sem,
    scatter_send,
    scatter_recv,
    ring_send,
    ring_recv,
    side_recv,
    cross_send,
    cross_recv,
    moved_send,
    moved_recv,
    part_send,
    part_recv,
    beside_send,
    beside_recv,
    late_send,
    late_recv,
    back_send,
    back_recv,
):
    bonds = lax.axis_size("bond")
    groups = lax.axis_size("mpo")
    me = lax.axis_index("bond")
    z = lax.axis_index("mpo")
    sectors = bonds // 2
    q = me // 2
    h = me % 2
    channels = left.shape[0]
    half = wave.shape[1] // 2
    rows = bonds * half
    cols = full.shape[-1]
    per_chunk = right.shape[1] // groups
    lines = bonds // PIECES
    turn = 1 - 2 * h
    partner = (me + turn, z)
    hops = groups // 2

    def chunk_at(offset):
        return (z + turn * offset + groups) % groups

    ahead = (me, chunk_at(1))
    behind = (me, chunk_at(-1))

    def parent(o):
        return 0 if abs(o) <= REACH else (REACH if o > 0 else -REACH)

    offsets = range(1 - hops, hops + 1)

    def children(o):
        return [c for c in offsets if abs(c) > 1 and parent(c) == o]

    far = [o for o in offsets if abs(o) > 1]
    pairs = [(hops, hops - 1), (1, -1), (1 - hops, 2), (-2, 0)]
    if hops == 2:
        pairs = [(2, 1), (-1, 0)]

    def remote(source, target, send, recv, device):
        return pltpu.make_async_remote_copy(
            src_ref=source,
            dst_ref=target,
            send_sem=send,
            recv_sem=recv,
            device_id=device,
            device_id_type=MESH,
        )

    def await_sent(block, sem):
        remote(block, block, sem, sem, partner).wait_send()

    right_own = right.at[:, :, h]
    load_left = pltpu.make_async_copy(left_env, left, local_sem.at[0])
    load_right = pltpu.make_async_copy(right_env, right_own, local_sem.at[1])
    swap_right = remote(right_env, right_own, pair_sem.at[0], pair_sem.at[1], partner)
    load_left.start()
    load_right.start()

    barrier = pltpu.get_barrier_semaphore()

    def greet(i, carry):
        pl.semaphore_signal(
            barrier, inc=1, device_id=((me + i) % bonds, z), device_id_type=MESH
        )
        return carry

    for distance in range(1, REACH + 1):
        for way in (distance, -distance):
            pl.semaphore_signal(
                barrier, inc=1, device_id=(me, chunk_at(way)), device_id_type=MESH
            )
    lax.fori_loop(1, bonds, greet, 0)
    pl.semaphore_wait(barrier, bonds - 1 + 2 * REACH)

    swap_right.start()

    def peer(i):
        return (me + jnp.where(i <= sectors, sectors - 1 + i, bonds - i)) % bonds

    def piece_of_wave(p, chunk):
        return wave.at[
            p // 2,
            pl.ds(pl.multiple_of((p % 2) * half, half), half),
            pl.ds(pl.multiple_of(chunk * cols, cols), cols),
        ]

    ours = [z % 2 + 2 * j for j in range(hops)]
    theirs = [1 - z % 2 + 2 * j for j in range(hops)]

    def scatter(j, i):
        p = peer(i)
        remote(
            piece_of_wave(p, ours[j]),
            start_in.at[j, me],
            scatter_send.at[0],
            scatter_recv.at[j],
            (p, z),
        ).start()

    def keep(j):
        return pltpu.make_async_copy(piece_of_wave(me, ours[j]), start_in.at[j, me], keep_sem.at[j])

    for j in range(hops):

        def spread(i, carry, j=j):
            scatter(j, i)
            return carry

        keep(j).start()
        lax.fori_loop(1, bonds, spread, 0)

    for step in range(2):
        for d, outside in ((0, 0), (1, sectors - 1)):

            @pl.when(q == outside)
            def _():
                moved_in[step, d] = jnp.zeros(moved_in.shape[2:], moved_in.dtype)
                late_in[step, d] = jnp.zeros(late_in.shape[2:], late_in.dtype)

    def live(first, count, chunk=z):
        row = lax.broadcasted_iota(jnp.int32, (count, cols), 0) + first
        col = lax.broadcasted_iota(jnp.int32, (count, cols), 1)
        row = (row // half) * (2 * half) + h * half + row % half
        return (row < left_sizes[q]) & (col + chunk * cols < right_sizes[q])

    def channel_of(shift):
        found = channels - 1
        for j in range(channels - 1):
            found = jnp.where(channel_shift[z * channels + j] == shift, j, found)
        return found

    order = [channel_of(1), channel_of(-1), channel_of(0)]

    def apply(step, carry):
        def line_set(chunk, piece):
            return full.at[step, chunk, pl.ds(piece * lines, lines), h]

        def pass_on(chunk, slot, piece, device):
            block = line_set(chunk, piece)
            return remote(block, block, ring_send.at[0], ring_recv.at[slot, piece], device)

        def share(chunk, piece):
            block = line_set(chunk, piece)
            return remote(
                block, block, cross_send.at[0], cross_recv.at[step, chunk, piece], partner
            )

        def mix_units(chunks):
            def unit(d):
                if d == 0:
                    for chunk in chunks:
                        for piece in range(PIECES):
                            share(chunk, piece).wait_recv()
                sets = [chunks]
                for some in sets:
                    vector = [full[step, chunk].reshape(2 * rows, cols) for chunk in some]
                    vector = vector[0] if len(vector) == 1 else jnp.concatenate(vector, axis=1)
                    block = jnp.dot(
                        left[order[d]], vector, preferred_element_type=jnp.float32
                    ).astype(mixed.dtype)
                    for n, chunk in enumerate(some):
                        mixed[d, :, pl.ds(pl.multiple_of(chunk * cols, cols), cols)] = block[
                            :, n * cols : (n + 1) * cols
                        ]

            return [lambda d=d: unit(d) for d in range(channels)]

        def run(queue, count=channels):
            for unit in queue[:count]:
                unit()
            del queue[:count]

        def to_side(j, chunk, way):
            block = full.at[0, chunk, :, h]
            return remote(
                block, block, ring_send.at[0], side_recv.at[j], (me, (z + way + groups) % groups)
            )

        def images(d, pair):
            blocks = [
                right[order[d], pl.ds(chunk * per_chunk, per_chunk)].reshape(cols, -1)
                for chunk in pair
            ]
            both = lax.dot_general(
                mixed[d],
                jnp.concatenate(blocks, axis=0),
                (((1,), (1,)), ((), ())),
                preferred_element_type=jnp.float32,
            )
            return both[:, :cols], both[:, cols:]

        has_target = [(q < sectors - 1), (q > 0)]
        has_source = [(q > 0), (q < sectors - 1)]

        def to_sector(d, o, device=partner):
            chunk = chunk_at(o)
            return remote(
                moved_out.at[d, chunk],
                moved_in.at[step, d, chunk],
                moved_send.at[d, o + hops - 1],
                moved_recv.at[step, d, o + hops - 1],
                device,
            )

        def late(d, device=partner):
            return remote(
                late_out.at[d], late_in.at[step, d], late_send.at[d], late_recv.at[step, d], device
            )

        def neighbour(d):
            return (me + (2 if d == 0 else -2), z)

        def to_beside(o, i):
            side = (1 - o) // 2
            source = moved_out.at[i, chunk_at(o)] if i < 2 else near_out.at[side]
            return remote(
                source,
                beside_in.at[step, side, i],
                beside_send.at[i // 2],
                beside_recv.at[step, side, i],
                (me, chunk_at(o)),
            )

        def partial(o):
            slot = o + hops - 1
            return remote(
                part_out.at[slot],
                part_in.at[step, slot],
                part_send.at[0],
                part_recv.at[step, slot],
                (me, chunk_at(o - parent(o))),
            )

        def add_children(o, total):
            for c in children(o):
                partial(c).wait_recv()
                total += part_in[step, c + hops - 1].astype(jnp.float32)
            return total

        def hop(o):
            chunk = chunk_at(o)
            total = near[chunk]
            for d in range(2):

                @pl.when(has_source[d])
                def _():
                    to_sector(d, o).wait_recv()

                total += moved_in[step, d, chunk].astype(jnp.float32)
            part_out[o + hops - 1] = add_children(o, total).astype(part_out.dtype)
            partial(o).start()

        def moved_pair(d, pair, offs):
            blocks = images(d, pair)
            for n, chunk in enumerate(pair):
                moved_out[d, chunk] = blocks[n].astype(moved_out.dtype)
            for u, some in offs:
                for o in some:
                    if o > REACH or hops == 2 and o == 2:

                        @pl.when(u & has_target[d])
                        def _():
                            to_sector(d, o, neighbour(d)).start()

                    if abs(o) == 1:

                        @pl.when(u)
                        def _():
                            to_beside(o, d).start()

        def near_pair(pair):
            near[pair[0]], near[pair[1]] = images(2, pair)

        def close(queue):
            pair = [chunk_at(o) for o in pairs[0]]
            for d in range(2):
                run(queue, 1)
                moved_pair(d, pair, [(True, pairs[0])])
            run(queue, 1)
            near_pair(pair)

        def image_pair(u, inner):
            first, second = pairs[-1]
            for t in range(1, len(pairs) - 1):
                first = jnp.where(u == t, pairs[t][0], first)
                second = jnp.where(u == t, pairs[t][1], second)
            pair = (chunk_at(first), chunk_at(second))
            for d in range(2):
                moved_pair(d, pair, [(u == t, pairs[t]) for t in range(1, len(pairs))])
            near_pair(pair)
            return inner

        @pl.when(step == 0)
        def _():
            def begin(j):
                keep(j).wait()
                others = start_in.at[j, pl.ds(0, bonds - 1)]
                remote(others, others, scatter_send.at[0], scatter_recv.at[j], partner).wait_recv()
                block = start_in[j].reshape(rows, cols)
                block = jnp.where(live(0, rows, ours[j]), block, jnp.zeros((), block.dtype))
                full[0, ours[j], :, h] = block.reshape(bonds, half, cols)
                to_side(j, ours[j], 1 - 2 * (j % 2)).start()
                for piece in range(PIECES):
                    share(ours[j], piece).start()

            def arrive(j):
                to_side(j, theirs[j], 1).wait_recv()
                for piece in range(PIECES):
                    share(theirs[j], piece).start()

            begin(0)
            begin(1)
            load_left.wait()
            queue = mix_units(ours[:2])
            for j in range(2, hops):
                begin(j)
                run(queue, 1)
            run(queue)
            queue = mix_units(ours[2:]) if hops > 2 else []
            for j in range(hops):
                arrive(j)
                run(queue, 1 + j % 2)
                if j % 2:
                    queue += mix_units(theirs[j - 1 : j + 1])
            run(queue, len(queue) - channels)
            load_right.wait()
            swap_right.wait()
            close(queue)
            sent = start_in.at[:, pl.ds(0, bonds - 1)]
            await_sent(sent, scatter_send.at[0])
            await_sent(full.at[0, pl.ds(0, hops), :, 0], ring_send.at[0])

        @pl.when(step == 1)
        def _():
            for piece in range(PIECES):
                pass_on(z, 0, piece, ahead).start()
                pass_on(z, 1, piece, behind).start()
            for piece in range(PIECES):
                share(z, piece).start()
            queue = mix_units([z])
            run(queue)
            for s in range(1, hops + 1):
                from_behind, from_ahead = chunk_at(-s), chunk_at(s)
                for piece in range(PIECES):
                    pass_on(from_behind, 2 * s - 2, piece, ahead).wait_recv()
                    if s < hops:
                        pass_on(from_behind, 2 * s, piece, ahead).start()
                    share(from_behind, piece).start()
                    if s < hops:
                        pass_on(from_ahead, 2 * s - 1, piece, behind).wait_recv()
                        if s < hops - 1:
                            pass_on(from_ahead, 2 * s + 1, piece, behind).start()
                        share(from_ahead, piece).start()
                    run(queue, 2 - piece)
                run(queue)
                queue = mix_units([from_behind, from_ahead] if s < hops else [from_behind])
            close(queue)
            await_sent(full.at[1, pl.ds(0, groups - 1), :, 0], ring_send.at[0])

        lax.fori_loop(1, len(pairs), image_pair, 0)

        @pl.when(step == 1)
        def _():
            send_back(first_out, full.at[1, z, :, h], 0)

        def send_after(o, done):
            for d in range(2):

                @pl.when(has_target[d])
                def _():
                    to_sector(d, done).wait_send()
                    if o:
                        to_sector(d, o, neighbour(d)).start()
                    else:
                        late(d, neighbour(d)).start()

        def merge_own():
            for d in range(2):
                moved = moved_out[d, z].astype(jnp.float32)
                for o in (1, -1):
                    to_beside(o, d).wait_recv()
                    moved += beside_in[step, (1 - o) // 2, d].astype(jnp.float32)
                late_out[d] = moved.astype(late_out.dtype)

        def send_beside():
            for o in (1, -1):
                near_out[(1 - o) // 2] = near[chunk_at(o)].astype(near_out.dtype)
                to_beside(o, 2).start()

        if hops == 2:
            send_beside()
            merge_own()
            send_after(0, 2)
            hop(2)
        else:
            send_after(-3, 4)
            hop(4)
            send_after(2, 3)
            hop(3)
            send_beside()
            send_after(-2, -3)
            hop(-3)
            merge_own()
            send_after(0, -2)
            hop(2)
            hop(-2)
            for d in range(2):

                @pl.when(has_target[d])
                def _():
                    to_sector(d, 2).wait_send()

        total = near[z]
        for o in (1, -1):
            to_beside(o, 2).wait_recv()
            total += beside_in[step, (1 - o) // 2, 2].astype(jnp.float32)
        total = add_children(0, total)
        for d in range(2):

            @pl.when(has_source[d])
            def _():
                late(d).wait_recv()

            total += late_in[step, d].astype(jnp.float32)

        def conclude(value, first, count):
            value = jnp.where(live(first, count), value, 0.0)
            span = pl.ds(first // half, count // half)
            shape = (count // half, half, cols)

            @pl.when(step == 0)
            def _():
                full[1, z, span, h] = value.astype(full.dtype).reshape(shape)

            @pl.when(step == 1)
            def _():
                begin = full[0, z, span, h].reshape(count, cols).astype(jnp.float32)
                last[span] = (2.0 * value - begin).astype(last.dtype).reshape(shape)

        conclude(total, 0, rows)

        for d in range(2):

            @pl.when(has_target[d])
            def _():
                late(d).wait_send()

        await_sent(moved_out.at[0, pl.ds(0, 4)], beside_send.at[0])
        await_sent(near_out, beside_send.at[1])
        await_sent(part_out.at[pl.ds(0, len(far))], part_send.at[0])
        await_sent(full.at[step, :, :, 0], cross_send.at[0])
        return carry

    def send_back(out, block, slot):
        def one(i, carry):
            p = peer(i)
            remote(
                block.at[p], out.at[q, h], back_send.at[slot], back_recv.at[slot], (p, z)
            ).start()
            return carry

        lax.fori_loop(1, bonds, one, 0)
        pltpu.make_async_copy(block.at[me], out.at[q, h], local_sem.at[2 + slot]).start()

    def finish(out, block, slot):
        pltpu.make_async_copy(block.at[me], out.at[q, h], local_sem.at[2 + slot]).wait()
        others = start_in.at[0, pl.ds(0, bonds - 1)]
        remote(others, others, back_send.at[slot], back_recv.at[slot], partner).wait()

    lax.fori_loop(0, 2, apply, 0)
    send_back(second_out, last, 1)
    finish(first_out, full.at[1, z, :, h], 0)
    finish(second_out, last, 1)


def hand_over(first, second, first_out, second_out):
    first_out[...] = first[...]
    second_out[...] = second[...]


def local(wavefunction, left_env, right_env, left_sizes, right_sizes, channel_shift):
    bonds = lax.axis_size("bond")
    groups = lax.axis_size("mpo")
    sectors, block_rows, states = wavefunction.shape
    half = block_rows // 2
    channels = left_env.shape[0]
    rows = bonds * half
    cols = states // groups
    dtype = wavefunction.dtype
    out = jax.ShapeDtypeStruct((sectors, 2, half, cols), dtype)
    dma = pltpu.SemaphoreType.DMA
    first, second = pl.pallas_call(
        kernel,
        out_shape=(out, out),
        in_specs=[pl.BlockSpec(memory_space=pl.ANY)] * 3
        + [pl.BlockSpec(memory_space=pltpu.SMEM)] * 3,
        out_specs=[pl.BlockSpec(memory_space=pl.ANY)] * 2,
        scratch_shapes=[
            pltpu.VMEM((channels, rows, states), dtype),
            pltpu.VMEM((channels, bonds, 2, half, states), dtype),
            pltpu.VMEM((groups // 2, bonds, half, cols), dtype),
            pltpu.VMEM((2, groups, bonds, 2, half, cols), dtype),
            pltpu.VMEM((channels, rows, states), dtype),
            pltpu.VMEM((groups, rows, cols), jnp.float32),
            pltpu.VMEM((2, groups, rows, cols), dtype),
            pltpu.VMEM((2, 2, groups, rows, cols), dtype),
            pltpu.VMEM((groups, rows, cols), dtype),
            pltpu.VMEM((2, groups, rows, cols), dtype),
            pltpu.VMEM((2, rows, cols), dtype),
            pltpu.VMEM((2, 2, 3, rows, cols), dtype),
            pltpu.VMEM((2, rows, cols), dtype),
            pltpu.VMEM((2, 2, rows, cols), dtype),
            pltpu.VMEM((bonds, half, cols), dtype),
            dma((4,)),
            dma((2,)),
            dma((groups // 2,)),
            dma((1,)),
            dma((groups // 2,)),
            dma((1,)),
            dma((groups - 1, PIECES)),
            dma((groups // 2,)),
            dma((1,)),
            dma((2, groups, PIECES)),
            dma((2, groups)),
            dma((2, 2, groups)),
            dma((1,)),
            dma((2, groups)),
            dma((2,)),
            dma((2, 2, 3)),
            dma((2,)),
            dma((2, 2)),
            dma((2,)),
            dma((2,)),
        ],
        compiler_params=pltpu.CompilerParams(
            collective_id=0, has_side_effects=True, vmem_limit_bytes=56 << 20
        ),
        cost_estimate=pl.CostEstimate(
            flops=8 * channels * rows * states * states,
            bytes_accessed=6 * channels * rows * states,
            transcendentals=0,
        ),
        name="two_steps",
    )(
        wavefunction,
        left_env.reshape(channels, rows, states),
        right_env.reshape(channels, bonds, half, states),
        left_sizes,
        right_sizes,
        channel_shift,
    )
    first, second = pl.pallas_call(hand_over, out_shape=(out, out), name="hand_over")(
        first, second
    )
    shape = (sectors, block_rows, cols)
    return first.reshape(shape), second.reshape(shape)


def solution(mesh):
    placed = (
        P(None, "bond", None),
        P("mpo", "bond", None, None),
        P("mpo", "bond", None, None),
        P(),
        P(),
        P(),
    )
    return jax.shard_map(
        local,
        mesh=mesh,
        in_specs=placed,
        out_specs=(P(None, "bond", "mpo"), P(None, "bond", "mpo")),
        check_vma=False,
    )
```

```python
import jax
import jax.numpy as jnp
from jax import lax
from jax.experimental import pallas as pl
from jax.experimental.pallas import tpu as pltpu
from jax.sharding import PartitionSpec as P

MESH = pl.DeviceIdType.MESH
PIECES = 2
Z_PART = 4
LAG = 2


def z_first_rows(rows):
    return max(16, rows * Z_PART // 512 * 16)


def kernel(
    wave,
    left_env,
    right_env,
    left_sizes,
    right_sizes,
    channel_shift,
    first_out,
    second_out,
    left,
    right,
    start_in,
    full,
    mixed,
    near,
    moved_out,
    moved_in,
    y_part_out,
    y_part_in,
    z_part_out,
    z_part_in,
    late_out,
    late_in,
    last,
    local_sem,
    pair_sem,
    keep_sem,
    scatter_send,
    scatter_recv,
    ring_send,
    ring_recv,
    side_recv,
    cross_send,
    cross_recv,
    moved_send,
    moved_recv,
    part_send,
    y_part_recv,
    z_part_recv,
    late_send,
    late_recv,
    back_send,
    back_recv,
):
    bonds = lax.axis_size("bond")
    groups = lax.axis_size("mpo")
    me = lax.axis_index("bond")
    z = lax.axis_index("mpo")
    sectors = bonds // 2
    q = me // 2
    h = me % 2
    channels = left.shape[0]
    half = wave.shape[1] // 2
    rows = bonds * half
    cols = full.shape[-1]
    per_chunk = right.shape[1] // groups
    lines = bonds // PIECES
    y_rows = moved_in.shape[3]
    z_rows = rows - y_rows
    y_span = pl.ds(0, y_rows)
    z_span = pl.ds(y_rows, z_rows)
    turn = 1 - 2 * h
    partner = (me + turn, z)
    hops = groups // 2

    def chunk_at(offset):
        return (z + turn * offset + groups) % groups

    ahead = (me, chunk_at(1))
    behind = (me, chunk_at(-1))
    reach = max(1, hops // 2)

    def parent(o):
        return 0 if abs(o) <= reach else (reach if o > 0 else -reach)

    offsets = range(1 - hops, hops + 1)

    def children(o):
        return [c for c in offsets if c and parent(c) == o]

    def remote(source, target, send, recv, device):
        return pltpu.make_async_remote_copy(
            src_ref=source,
            dst_ref=target,
            send_sem=send,
            recv_sem=recv,
            device_id=device,
            device_id_type=MESH,
        )

    def await_sent(block, sem):
        remote(block, block, sem, sem, partner).wait_send()

    right_own = right.at[:, :, h]
    load_left = pltpu.make_async_copy(left_env, left, local_sem.at[0])
    load_right = pltpu.make_async_copy(right_env, right_own, local_sem.at[1])
    swap_right = remote(right_env, right_own, pair_sem.at[0], pair_sem.at[1], partner)
    load_left.start()
    load_right.start()

    barrier = pltpu.get_barrier_semaphore()

    def greet(i, carry):
        pl.semaphore_signal(
            barrier, inc=1, device_id=((me + i) % bonds, z), device_id_type=MESH
        )
        return carry

    for distance in range(1, reach + 1):
        for way in (distance, -distance):
            pl.semaphore_signal(
                barrier, inc=1, device_id=(me, chunk_at(way)), device_id_type=MESH
            )
    lax.fori_loop(1, bonds, greet, 0)
    pl.semaphore_wait(barrier, bonds - 1 + 2 * reach)

    swap_right.start()

    def piece_of_wave(p, chunk):
        return wave.at[
            p // 2,
            pl.ds(pl.multiple_of((p % 2) * half, half), half),
            pl.ds(pl.multiple_of(chunk * cols, cols), cols),
        ]

    ours = [z % 2 + 2 * j for j in range(hops)]
    theirs = [1 - z % 2 + 2 * j for j in range(hops)]

    def scatter(j, i):
        p = (me + i) % bonds
        remote(
            piece_of_wave(p, ours[j]),
            start_in.at[j, me],
            scatter_send.at[0],
            scatter_recv.at[j],
            (p, z),
        ).start()

    def keep(j):
        return pltpu.make_async_copy(piece_of_wave(me, ours[j]), start_in.at[j, me], keep_sem.at[j])

    for j in range(hops):

        def spread(i, carry, j=j):
            scatter(j, i)
            return carry

        keep(j).start()
        lax.fori_loop(1, bonds, spread, 0)

    for step in range(2):
        for d, outside in ((0, 0), (1, sectors - 1)):

            @pl.when(q == outside)
            def _():
                moved_in[step, d] = jnp.zeros(moved_in.shape[2:], moved_in.dtype)
                late_in[step, d] = jnp.zeros(late_in.shape[2:], late_in.dtype)

    def live(first, count, chunk=z):
        row = lax.broadcasted_iota(jnp.int32, (count, cols), 0) + first
        col = lax.broadcasted_iota(jnp.int32, (count, cols), 1)
        row = (row // half) * (2 * half) + h * half + row % half
        return (row < left_sizes[q]) & (col + chunk * cols < right_sizes[q])

    def channel_of(shift):
        found = channels - 1
        for j in range(channels - 1):
            found = jnp.where(channel_shift[z * channels + j] == shift, j, found)
        return found

    order = [channel_of(1), channel_of(-1), channel_of(0)]

    def apply(step, carry):
        def line_set(chunk, piece):
            return full.at[step, chunk, pl.ds(piece * lines, lines), h]

        def pass_on(chunk, slot, piece, device):
            block = line_set(chunk, piece)
            return remote(block, block, ring_send.at[0], ring_recv.at[slot, piece], device)

        def share(chunk, piece):
            block = line_set(chunk, piece)
            return remote(
                block, block, cross_send.at[0], cross_recv.at[step, chunk, piece], partner
            )

        def mix_units(chunks):
            def unit(d):
                if d == 0:
                    for chunk in chunks:
                        for piece in range(PIECES):
                            share(chunk, piece).wait_recv()
                sets = [chunks]
                for some in sets:
                    vector = [full[step, chunk].reshape(2 * rows, cols) for chunk in some]
                    vector = vector[0] if len(vector) == 1 else jnp.concatenate(vector, axis=1)
                    block = jnp.dot(
                        left[order[d]], vector, preferred_element_type=jnp.float32
                    ).astype(mixed.dtype)
                    for n, chunk in enumerate(some):
                        mixed[d, :, pl.ds(pl.multiple_of(chunk * cols, cols), cols)] = block[
                            :, n * cols : (n + 1) * cols
                        ]

            return [lambda d=d: unit(d) for d in range(channels)]

        def run(queue, count=channels):
            for unit in queue[:count]:
                unit()
            del queue[:count]

        def to_side(j, chunk, way):
            block = full.at[0, chunk, :, h]
            return remote(
                block, block, ring_send.at[0], side_recv.at[j], (me, (z + way + groups) % groups)
            )

        @pl.when(step == 0)
        def _():
            def begin(j):
                keep(j).wait()
                others = start_in.at[j, pl.ds(0, bonds - 1)]
                remote(others, others, scatter_send.at[0], scatter_recv.at[j], partner).wait_recv()
                block = start_in[j].reshape(rows, cols)
                block = jnp.where(live(0, rows, ours[j]), block, jnp.zeros((), block.dtype))
                full[0, ours[j], :, h] = block.reshape(bonds, half, cols)
                to_side(j, ours[j], 1 - 2 * (j % 2)).start()
                for piece in range(PIECES):
                    share(ours[j], piece).start()

            def arrive(j):
                to_side(j, theirs[j], 1).wait_recv()
                for piece in range(PIECES):
                    share(theirs[j], piece).start()

            begin(0)
            begin(1)
            load_left.wait()
            queue = mix_units(ours[:2])
            for j in range(2, hops):
                begin(j)
                run(queue, 1)
            run(queue)
            queue = mix_units(ours[2:]) if hops > 2 else []
            for j in range(hops):
                arrive(j)
                run(queue, 1 + j % 2)
                if j % 2:
                    queue += mix_units(theirs[j - 1 : j + 1])
            run(queue, len(queue))
            sent = start_in.at[:, pl.ds(0, bonds - 1)]
            await_sent(sent, scatter_send.at[0])
            await_sent(full.at[0, pl.ds(0, hops), :, 0], ring_send.at[0])
            load_right.wait()
            swap_right.wait()

        @pl.when(step == 1)
        def _():
            for piece in range(PIECES):
                pass_on(z, 0, piece, ahead).start()
                pass_on(z, 1, piece, behind).start()
            for piece in range(PIECES):
                share(z, piece).start()
            send_back(first_out, full.at[1, z, :, h], 0)
            queue = mix_units([z])
            run(queue)
            for s in range(1, hops + 1):
                from_behind, from_ahead = chunk_at(-s), chunk_at(s)
                for piece in range(PIECES):
                    pass_on(from_behind, 2 * s - 2, piece, ahead).wait_recv()
                    if s < hops:
                        pass_on(from_behind, 2 * s, piece, ahead).start()
                    share(from_behind, piece).start()
                    if s < hops:
                        pass_on(from_ahead, 2 * s - 1, piece, behind).wait_recv()
                        if s < hops - 1:
                            pass_on(from_ahead, 2 * s + 1, piece, behind).start()
                        share(from_ahead, piece).start()
                    run(queue, 2 - piece)
                run(queue)
                queue = mix_units([from_behind, from_ahead] if s < hops else [from_behind])
            run(queue)
            await_sent(full.at[1, pl.ds(0, groups - 1), :, 0], ring_send.at[0])

        def images(d, pair):
            blocks = [
                right[order[d], pl.ds(chunk * per_chunk, per_chunk)].reshape(cols, -1)
                for chunk in pair
            ]
            both = lax.dot_general(
                mixed[d],
                jnp.concatenate(blocks, axis=0),
                (((1,), (1,)), ((), ())),
                preferred_element_type=jnp.float32,
            )
            return both[:, :cols], both[:, cols:]

        has_target = [(q < sectors - 1), (q > 0)]
        has_source = [(q > 0), (q < sectors - 1)]

        def to_sector(d, chunk, k, device=partner):
            return remote(
                moved_out.at[d, chunk, y_span],
                moved_in.at[step, d, chunk],
                moved_send.at[d],
                moved_recv.at[step, d, k],
                device,
            )

        def late(d, device=partner):
            return remote(
                late_out.at[d], late_in.at[step, d], late_send.at[d], late_recv.at[step, d], device
            )

        def neighbour(d):
            return (me + (2 if d == 0 else -2), z)

        def z_partial(o):
            slot = o + hops - 1
            return remote(
                z_part_out.at[slot],
                z_part_in.at[step, slot],
                part_send.at[0],
                z_part_recv.at[step, slot],
                (me, chunk_at(o - parent(o))),
            )

        def y_partial(o):
            slot = o + hops - 1
            return remote(
                y_part_out.at[slot],
                y_part_in.at[step, slot],
                part_send.at[1],
                y_part_recv.at[step, slot],
                (me, chunk_at(o - parent(o))),
            )

        def z_terms(chunk):
            return [
                near[chunk, z_span],
                moved_out[0, chunk, z_span].astype(jnp.float32),
                moved_out[1, chunk, z_span].astype(jnp.float32),
            ]

        def y_terms(chunk, part=y_span):
            return (
                near[chunk, part]
                + moved_in[step, 0, chunk, part].astype(jnp.float32)
                + moved_in[step, 1, chunk, part].astype(jnp.float32)
            )

        def await_moved(k, chunk):
            for d in range(2):

                @pl.when(has_source[d])
                def _():
                    to_sector(d, chunk, k).wait_recv()

        def z_sum(o):
            terms = z_terms(chunk_at(o))
            for c in children(o):
                z_partial(c).wait_recv()
                for i in range(3):
                    terms[i] += z_part_in[step, c + hops - 1, i].astype(jnp.float32)
            return terms

        def z_hop(o):
            for i, term in enumerate(z_sum(o)):
                z_part_out[o + hops - 1, i] = term.astype(z_part_out.dtype)
            z_partial(o).start()

        def y_sum(o, k):
            await_moved(k, chunk_at(o))
            total = y_terms(chunk_at(o))
            for c in children(o):
                y_partial(c).wait_recv()
                total += y_part_in[step, c + hops - 1].astype(jnp.float32)
            return total

        def y_hop(o, k):
            y_part_out[o + hops - 1] = y_sum(o, k).astype(y_part_out.dtype)
            y_partial(o).start()

        pairs = [(hops if t == 0 else t - hops, hops - 1 - t) for t in range(hops)]

        def round_of_tree(u, inner):
            @pl.when(u < hops)
            def _():
                pair = (
                    chunk_at(jnp.where(u == 0, hops, u - hops)),
                    chunk_at(hops - 1 - u),
                )
                for d in range(2):
                    blocks = images(d, pair)
                    for n, chunk in enumerate(pair):
                        moved_out[d, chunk] = blocks[n].astype(moved_out.dtype)

                        @pl.when(has_target[d])
                        def _():
                            to_sector(d, chunk, 2 * u + n, neighbour(d)).start()

                near[pair[0]], near[pair[1]] = images(2, pair)

            for t in range(hops):

                @pl.when(u == t)
                def _():
                    for o in pairs[t]:
                        if o and not children(o):
                            z_hop(o)

            @pl.when(u == hops - 1)
            def _():
                for o in offsets:
                    if o and children(o):
                        z_hop(o)

            @pl.when(u == hops - 1 + LAG)
            def _():
                for i, term in enumerate(z_sum(0)):
                    if i == 0:
                        near[z, z_span] = term
                    else:
                        late_out[i - 1] = term.astype(late_out.dtype)

                        @pl.when(has_target[i - 1])
                        def _():
                            late(i - 1, neighbour(i - 1)).start()

            for t in range(hops):

                @pl.when(u == t + LAG)
                def _():
                    for n, o in enumerate(pairs[t]):
                        if o:
                            y_hop(o, 2 * t + n)

            return inner

        lax.fori_loop(0, hops + LAG, round_of_tree, 0)

        def conclude(value, first, count):
            value = jnp.where(live(first, count), value, 0.0)
            span = pl.ds(first // half, count // half)
            shape = (count // half, half, cols)

            @pl.when(step == 0)
            def _():
                full[1, z, span, h] = value.astype(full.dtype).reshape(shape)

            @pl.when(step == 1)
            def _():
                begin = full[0, z, span, h].reshape(count, cols).astype(jnp.float32)
                last[span] = (2.0 * value - begin).astype(last.dtype).reshape(shape)

        conclude(y_sum(0, groups - 1), 0, y_rows)
        for d in range(2):

            @pl.when(has_source[d])
            def _():
                late(d).wait_recv()

        total = (
            near[z, z_span]
            + late_in[step, 0].astype(jnp.float32)
            + late_in[step, 1].astype(jnp.float32)
        )
        conclude(total, y_rows, z_rows)

        for d in range(2):

            @pl.when(has_target[d])
            def _():
                await_sent(moved_out.at[d, :, y_span], moved_send.at[d])
                late(d).wait_send()

        await_sent(z_part_out.at[pl.ds(0, groups - 1)], part_send.at[0])
        await_sent(y_part_out.at[pl.ds(0, groups - 1)], part_send.at[1])
        await_sent(full.at[step, :, :, 0], cross_send.at[0])
        return carry

    def send_back(out, block, slot):
        def one(i, carry):
            p = (me + i) % bonds
            remote(
                block.at[p], out.at[q, h], back_send.at[slot], back_recv.at[slot], (p, z)
            ).start()
            return carry

        lax.fori_loop(1, bonds, one, 0)
        pltpu.make_async_copy(block.at[me], out.at[q, h], local_sem.at[2 + slot]).start()

    def finish(out, block, slot):
        pltpu.make_async_copy(block.at[me], out.at[q, h], local_sem.at[2 + slot]).wait()
        others = start_in.at[0, pl.ds(0, bonds - 1)]
        remote(others, others, back_send.at[slot], back_recv.at[slot], partner).wait()

    lax.fori_loop(0, 2, apply, 0)
    send_back(second_out, last, 1)
    finish(first_out, full.at[1, z, :, h], 0)
    finish(second_out, last, 1)


def hand_over(first, second, first_out, second_out):
    first_out[...] = first[...]
    second_out[...] = second[...]


def local(wavefunction, left_env, right_env, left_sizes, right_sizes, channel_shift):
    bonds = lax.axis_size("bond")
    groups = lax.axis_size("mpo")
    sectors, block_rows, states = wavefunction.shape
    half = block_rows // 2
    channels = left_env.shape[0]
    rows = bonds * half
    cols = states // groups
    z_rows = z_first_rows(rows)
    y_rows = rows - z_rows
    dtype = wavefunction.dtype
    out = jax.ShapeDtypeStruct((sectors, 2, half, cols), dtype)
    dma = pltpu.SemaphoreType.DMA
    first, second = pl.pallas_call(
        kernel,
        out_shape=(out, out),
        in_specs=[pl.BlockSpec(memory_space=pl.ANY)] * 3
        + [pl.BlockSpec(memory_space=pltpu.SMEM)] * 3,
        out_specs=[pl.BlockSpec(memory_space=pl.ANY)] * 2,
        scratch_shapes=[
            pltpu.VMEM((channels, rows, states), dtype),
            pltpu.VMEM((channels, bonds, 2, half, states), dtype),
            pltpu.VMEM((groups // 2, bonds, half, cols), dtype),
            pltpu.VMEM((2, groups, bonds, 2, half, cols), dtype),
            pltpu.VMEM((channels, rows, states), dtype),
            pltpu.VMEM((groups, rows, cols), jnp.float32),
            pltpu.VMEM((2, groups, rows, cols), dtype),
            pltpu.VMEM((2, 2, groups, y_rows, cols), dtype),
            pltpu.VMEM((groups, y_rows, cols), dtype),
            pltpu.VMEM((2, groups, y_rows, cols), dtype),
            pltpu.VMEM((groups, 3, z_rows, cols), dtype),
            pltpu.VMEM((2, groups, 3, z_rows, cols), dtype),
            pltpu.VMEM((2, z_rows, cols), dtype),
            pltpu.VMEM((2, 2, z_rows, cols), dtype),
            pltpu.VMEM((bonds, half, cols), dtype),
            dma((4,)),
            dma((2,)),
            dma((groups // 2,)),
            dma((1,)),
            dma((groups // 2,)),
            dma((1,)),
            dma((groups - 1, PIECES)),
            dma((groups // 2,)),
            dma((1,)),
            dma((2, groups, PIECES)),
            dma((2,)),
            dma((2, 2, groups)),
            dma((2,)),
            dma((2, groups)),
            dma((2, groups)),
            dma((2,)),
            dma((2, 2)),
            dma((2,)),
            dma((2,)),
        ],
        compiler_params=pltpu.CompilerParams(
            collective_id=0, has_side_effects=True, vmem_limit_bytes=56 << 20
        ),
        cost_estimate=pl.CostEstimate(
            flops=8 * channels * rows * states * states,
            bytes_accessed=6 * channels * rows * states,
            transcendentals=0,
        ),
        name="two_steps",
    )(
        wavefunction,
        left_env.reshape(channels, rows, states),
        right_env.reshape(channels, bonds, half, states),
        left_sizes,
        right_sizes,
        channel_shift,
    )
    first, second = pl.pallas_call(hand_over, out_shape=(out, out), name="hand_over")(
        first, second
    )
    shape = (sectors, block_rows, cols)
    return first.reshape(shape), second.reshape(shape)


def solution(mesh):
    placed = (
        P(None, "bond", None),
        P("mpo", "bond", None, None),
        P("mpo", "bond", None, None),
        P(),
        P(),
        P(),
    )
    return jax.shard_map(
        local,
        mesh=mesh,
        in_specs=placed,
        out_specs=(P(None, "bond", "mpo"), P(None, "bond", "mpo")),
        check_vma=False,
    )
```

```python
import jax
import jax.numpy as jnp
from jax import lax
from jax.experimental import pallas as pl
from jax.experimental.pallas import tpu as pltpu
from jax.sharding import PartitionSpec as P

MESH = pl.DeviceIdType.MESH
PIECES = 2
Z_PART = 4
LAG = 2
SPLIT = 2


def z_first_rows(rows):
    return max(16, rows * Z_PART // 512 * 16)


def kernel(
    wave,
    left_env,
    right_env,
    left_sizes,
    right_sizes,
    channel_shift,
    first_out,
    second_out,
    left,
    right,
    start_in,
    full,
    mixed,
    near,
    moved_out,
    moved_in,
    y_part_out,
    y_part_in,
    z_part_out,
    z_part_in,
    late_out,
    late_in,
    last,
    local_sem,
    pair_sem,
    keep_sem,
    scatter_send,
    scatter_recv,
    ring_send,
    ring_recv,
    side_recv,
    cross_send,
    cross_recv,
    moved_send,
    moved_recv,
    part_send,
    y_part_recv,
    z_part_recv,
    late_send,
    late_recv,
    back_send,
    back_recv,
):
    bonds = lax.axis_size("bond")
    groups = lax.axis_size("mpo")
    me = lax.axis_index("bond")
    z = lax.axis_index("mpo")
    sectors = bonds // 2
    q = me // 2
    h = me % 2
    channels = left.shape[0]
    half = wave.shape[1] // 2
    rows = bonds * half
    cols = full.shape[-1]
    per_chunk = right.shape[1] // groups
    lines = bonds // PIECES
    y_rows = moved_in.shape[3]
    z_rows = rows - y_rows
    y_span = pl.ds(0, y_rows)
    z_span = pl.ds(y_rows, z_rows)
    turn = 1 - 2 * h
    partner = (me + turn, z)
    hops = groups // 2

    def chunk_at(offset):
        return (z + turn * offset + groups) % groups

    ahead = (me, chunk_at(1))
    behind = (me, chunk_at(-1))
    reach = max(1, hops // 2)

    def parent(o):
        return 0 if abs(o) <= reach else (reach if o > 0 else -reach)

    offsets = range(1 - hops, hops + 1)

    def children(o):
        return [c for c in offsets if c and parent(c) == o]

    def remote(source, target, send, recv, device):
        return pltpu.make_async_remote_copy(
            src_ref=source,
            dst_ref=target,
            send_sem=send,
            recv_sem=recv,
            device_id=device,
            device_id_type=MESH,
        )

    def await_sent(block, sem):
        remote(block, block, sem, sem, partner).wait_send()

    right_own = right.at[:, :, h]
    load_left = pltpu.make_async_copy(left_env, left, local_sem.at[0])
    load_right = pltpu.make_async_copy(right_env, right_own, local_sem.at[1])
    swap_right = remote(right_env, right_own, pair_sem.at[0], pair_sem.at[1], partner)
    load_left.start()
    load_right.start()

    barrier = pltpu.get_barrier_semaphore()

    def greet(i, carry):
        pl.semaphore_signal(
            barrier, inc=1, device_id=((me + i) % bonds, z), device_id_type=MESH
        )
        return carry

    for distance in range(1, reach + 1):
        for way in (distance, -distance):
            pl.semaphore_signal(
                barrier, inc=1, device_id=(me, chunk_at(way)), device_id_type=MESH
            )
    lax.fori_loop(1, bonds, greet, 0)
    pl.semaphore_wait(barrier, bonds - 1 + 2 * reach)

    swap_right.start()

    def piece_of_wave(p, chunk):
        return wave.at[
            p // 2,
            pl.ds(pl.multiple_of((p % 2) * half, half), half),
            pl.ds(pl.multiple_of(chunk * cols, cols), cols),
        ]

    ours = [z % 2 + 2 * j for j in range(hops)]
    theirs = [1 - z % 2 + 2 * j for j in range(hops)]

    def scatter(j, i):
        p = (me + i) % bonds
        remote(
            piece_of_wave(p, ours[j]),
            start_in.at[j, me],
            scatter_send.at[0],
            scatter_recv.at[j],
            (p, z),
        ).start()

    def keep(j):
        return pltpu.make_async_copy(piece_of_wave(me, ours[j]), start_in.at[j, me], keep_sem.at[j])

    for j in range(hops):

        def spread(i, carry, j=j):
            scatter(j, i)
            return carry

        keep(j).start()
        lax.fori_loop(1, bonds, spread, 0)

    for step in range(2):
        for d, outside in ((0, 0), (1, sectors - 1)):

            @pl.when(q == outside)
            def _():
                moved_in[step, d] = jnp.zeros(moved_in.shape[2:], moved_in.dtype)
                late_in[step, d] = jnp.zeros(late_in.shape[2:], late_in.dtype)

    def live(first, count, chunk=z):
        row = lax.broadcasted_iota(jnp.int32, (count, cols), 0) + first
        col = lax.broadcasted_iota(jnp.int32, (count, cols), 1)
        row = (row // half) * (2 * half) + h * half + row % half
        return (row < left_sizes[q]) & (col + chunk * cols < right_sizes[q])

    def channel_of(shift):
        found = channels - 1
        for j in range(channels - 1):
            found = jnp.where(channel_shift[z * channels + j] == shift, j, found)
        return found

    order = [channel_of(1), channel_of(-1), channel_of(0)]

    def apply(step, carry):
        def line_set(chunk, piece):
            return full.at[step, chunk, pl.ds(piece * lines, lines), h]

        def pass_on(chunk, slot, piece, device):
            block = line_set(chunk, piece)
            return remote(block, block, ring_send.at[0], ring_recv.at[slot, piece], device)

        def share(chunk, piece):
            block = line_set(chunk, piece)
            return remote(
                block, block, cross_send.at[0], cross_recv.at[step, chunk, piece], partner
            )

        def mix_units(chunks):
            def unit(d):
                if d == 0:
                    for chunk in chunks:
                        for piece in range(PIECES):
                            share(chunk, piece).wait_recv()
                sets = [chunks]
                for some in sets:
                    vector = [full[step, chunk].reshape(2 * rows, cols) for chunk in some]
                    vector = vector[0] if len(vector) == 1 else jnp.concatenate(vector, axis=1)
                    block = jnp.dot(
                        left[order[d]], vector, preferred_element_type=jnp.float32
                    ).astype(mixed.dtype)
                    for n, chunk in enumerate(some):
                        mixed[d, :, pl.ds(pl.multiple_of(chunk * cols, cols), cols)] = block[
                            :, n * cols : (n + 1) * cols
                        ]

            return [lambda d=d: unit(d) for d in range(channels)]

        def run(queue, count=channels):
            for unit in queue[:count]:
                unit()
            del queue[:count]

        def to_side(j, chunk, way):
            block = full.at[0, chunk, :, h]
            return remote(
                block, block, ring_send.at[0], side_recv.at[j], (me, (z + way + groups) % groups)
            )

        @pl.when(step == 0)
        def _():
            def begin(j):
                keep(j).wait()
                others = start_in.at[j, pl.ds(0, bonds - 1)]
                remote(others, others, scatter_send.at[0], scatter_recv.at[j], partner).wait_recv()
                block = start_in[j].reshape(rows, cols)
                block = jnp.where(live(0, rows, ours[j]), block, jnp.zeros((), block.dtype))
                full[0, ours[j], :, h] = block.reshape(bonds, half, cols)
                to_side(j, ours[j], 1 - 2 * (j % 2)).start()
                for piece in range(PIECES):
                    share(ours[j], piece).start()

            def arrive(j):
                to_side(j, theirs[j], 1).wait_recv()
                for piece in range(PIECES):
                    share(theirs[j], piece).start()

            begin(0)
            begin(1)
            load_left.wait()
            queue = mix_units(ours[:2])
            for j in range(2, hops):
                begin(j)
                run(queue, 1)
            run(queue)
            queue = mix_units(ours[2:]) if hops > 2 else []
            for j in range(hops):
                arrive(j)
                run(queue, 1 + j % 2)
                if j % 2:
                    queue += mix_units(theirs[j - 1 : j + 1])
            run(queue, len(queue))
            sent = start_in.at[:, pl.ds(0, bonds - 1)]
            await_sent(sent, scatter_send.at[0])
            await_sent(full.at[0, pl.ds(0, hops), :, 0], ring_send.at[0])
            load_right.wait()
            swap_right.wait()

        @pl.when(step == 1)
        def _():
            for piece in range(PIECES):
                pass_on(z, 0, piece, ahead).start()
                pass_on(z, 1, piece, behind).start()
            for piece in range(PIECES):
                share(z, piece).start()
            send_back(first_out, full.at[1, z, :, h], 0)
            queue = mix_units([z])
            run(queue)
            for s in range(1, hops + 1):
                from_behind, from_ahead = chunk_at(-s), chunk_at(s)
                for piece in range(PIECES):
                    pass_on(from_behind, 2 * s - 2, piece, ahead).wait_recv()
                    if s < hops:
                        pass_on(from_behind, 2 * s, piece, ahead).start()
                    share(from_behind, piece).start()
                    if s < hops:
                        pass_on(from_ahead, 2 * s - 1, piece, behind).wait_recv()
                        if s < hops - 1:
                            pass_on(from_ahead, 2 * s + 1, piece, behind).start()
                        share(from_ahead, piece).start()
                    run(queue, 2 - piece)
                run(queue)
                queue = mix_units([from_behind, from_ahead] if s < hops else [from_behind])
            run(queue)
            await_sent(full.at[1, pl.ds(0, groups - 1), :, 0], ring_send.at[0])

        def images(d, pair):
            blocks = [
                right[order[d], pl.ds(chunk * per_chunk, per_chunk)].reshape(cols, -1)
                for chunk in pair
            ]
            block = jnp.concatenate(blocks, axis=0)
            share_rows = rows // SPLIT
            both = [
                lax.dot_general(
                    mixed[d, n * share_rows : (n + 1) * share_rows],
                    block,
                    (((1,), (1,)), ((), ())),
                    preferred_element_type=jnp.float32,
                )
                for n in range(SPLIT)
            ]
            both = jnp.concatenate(both, axis=0)
            return both[:, :cols], both[:, cols:]

        has_target = [(q < sectors - 1), (q > 0)]
        has_source = [(q > 0), (q < sectors - 1)]

        def to_sector(d, chunk, k, device=partner):
            return remote(
                moved_out.at[d, chunk, y_span],
                moved_in.at[step, d, chunk],
                moved_send.at[d],
                moved_recv.at[step, d, k],
                device,
            )

        def late(d, device=partner):
            return remote(
                late_out.at[d], late_in.at[step, d], late_send.at[d], late_recv.at[step, d], device
            )

        def neighbour(d):
            return (me + (2 if d == 0 else -2), z)

        def z_partial(o):
            slot = o + hops - 1
            return remote(
                z_part_out.at[slot],
                z_part_in.at[step, slot],
                part_send.at[0],
                z_part_recv.at[step, slot],
                (me, chunk_at(o - parent(o))),
            )

        def y_partial(o):
            slot = o + hops - 1
            return remote(
                y_part_out.at[slot],
                y_part_in.at[step, slot],
                part_send.at[1],
                y_part_recv.at[step, slot],
                (me, chunk_at(o - parent(o))),
            )

        def z_terms(chunk):
            return [
                near[chunk, z_span],
                moved_out[0, chunk, z_span].astype(jnp.float32),
                moved_out[1, chunk, z_span].astype(jnp.float32),
            ]

        def y_terms(chunk, part=y_span):
            return (
                near[chunk, part]
                + moved_in[step, 0, chunk, part].astype(jnp.float32)
                + moved_in[step, 1, chunk, part].astype(jnp.float32)
            )

        def await_moved(k, chunk):
            for d in range(2):

                @pl.when(has_source[d])
                def _():
                    to_sector(d, chunk, k).wait_recv()

        def z_sum(o):
            terms = z_terms(chunk_at(o))
            for c in children(o):
                z_partial(c).wait_recv()
                for i in range(3):
                    terms[i] += z_part_in[step, c + hops - 1, i].astype(jnp.float32)
            return terms

        def z_hop(o):
            for i, term in enumerate(z_sum(o)):
                z_part_out[o + hops - 1, i] = term.astype(z_part_out.dtype)
            z_partial(o).start()

        def y_sum(o, k):
            await_moved(k, chunk_at(o))
            total = y_terms(chunk_at(o))
            for c in children(o):
                y_partial(c).wait_recv()
                total += y_part_in[step, c + hops - 1].astype(jnp.float32)
            return total

        def y_hop(o, k):
            y_part_out[o + hops - 1] = y_sum(o, k).astype(y_part_out.dtype)
            y_partial(o).start()

        pairs = [(hops if t == 0 else t - hops, hops - 1 - t) for t in range(hops)]

        def round_of_tree(u, inner):
            @pl.when(u < hops)
            def _():
                pair = (
                    chunk_at(jnp.where(u == 0, hops, u - hops)),
                    chunk_at(hops - 1 - u),
                )
                for d in range(2):
                    blocks = images(d, pair)
                    for n, chunk in enumerate(pair):
                        moved_out[d, chunk] = blocks[n].astype(moved_out.dtype)

                        @pl.when(has_target[d])
                        def _():
                            to_sector(d, chunk, 2 * u + n, neighbour(d)).start()

                near[pair[0]], near[pair[1]] = images(2, pair)

            for t in range(hops):

                @pl.when(u == t)
                def _():
                    for o in pairs[t]:
                        if o and not children(o):
                            z_hop(o)

            @pl.when(u == hops - 1)
            def _():
                for o in offsets:
                    if o and children(o):
                        z_hop(o)

            @pl.when(u == hops - 1 + LAG)
            def _():
                for i, term in enumerate(z_sum(0)):
                    if i == 0:
                        near[z, z_span] = term
                    else:
                        late_out[i - 1] = term.astype(late_out.dtype)

                        @pl.when(has_target[i - 1])
                        def _():
                            late(i - 1, neighbour(i - 1)).start()

            for t in range(hops):

                @pl.when(u == t + LAG)
                def _():
                    for n, o in enumerate(pairs[t]):
                        if o:
                            y_hop(o, 2 * t + n)

            return inner

        lax.fori_loop(0, hops + LAG, round_of_tree, 0)

        def conclude(value, first, count):
            value = jnp.where(live(first, count), value, 0.0)
            span = pl.ds(first // half, count // half)
            shape = (count // half, half, cols)

            @pl.when(step == 0)
            def _():
                full[1, z, span, h] = value.astype(full.dtype).reshape(shape)

            @pl.when(step == 1)
            def _():
                begin = full[0, z, span, h].reshape(count, cols).astype(jnp.float32)
                last[span] = (2.0 * value - begin).astype(last.dtype).reshape(shape)

        conclude(y_sum(0, groups - 1), 0, y_rows)
        for d in range(2):

            @pl.when(has_source[d])
            def _():
                late(d).wait_recv()

        total = (
            near[z, z_span]
            + late_in[step, 0].astype(jnp.float32)
            + late_in[step, 1].astype(jnp.float32)
        )
        conclude(total, y_rows, z_rows)

        for d in range(2):

            @pl.when(has_target[d])
            def _():
                await_sent(moved_out.at[d, :, y_span], moved_send.at[d])
                late(d).wait_send()

        await_sent(z_part_out.at[pl.ds(0, groups - 1)], part_send.at[0])
        await_sent(y_part_out.at[pl.ds(0, groups - 1)], part_send.at[1])
        await_sent(full.at[step, :, :, 0], cross_send.at[0])
        return carry

    def send_back(out, block, slot):
        def one(i, carry):
            p = (me + i) % bonds
            remote(
                block.at[p], out.at[q, h], back_send.at[slot], back_recv.at[slot], (p, z)
            ).start()
            return carry

        lax.fori_loop(1, bonds, one, 0)
        pltpu.make_async_copy(block.at[me], out.at[q, h], local_sem.at[2 + slot]).start()

    def finish(out, block, slot):
        pltpu.make_async_copy(block.at[me], out.at[q, h], local_sem.at[2 + slot]).wait()
        others = start_in.at[0, pl.ds(0, bonds - 1)]
        remote(others, others, back_send.at[slot], back_recv.at[slot], partner).wait()

    lax.fori_loop(0, 2, apply, 0)
    send_back(second_out, last, 1)
    finish(first_out, full.at[1, z, :, h], 0)
    finish(second_out, last, 1)


def hand_over(first, second, first_out, second_out):
    first_out[...] = first[...]
    second_out[...] = second[...]


def local(wavefunction, left_env, right_env, left_sizes, right_sizes, channel_shift):
    bonds = lax.axis_size("bond")
    groups = lax.axis_size("mpo")
    sectors, block_rows, states = wavefunction.shape
    half = block_rows // 2
    channels = left_env.shape[0]
    rows = bonds * half
    cols = states // groups
    z_rows = z_first_rows(rows)
    y_rows = rows - z_rows
    dtype = wavefunction.dtype
    out = jax.ShapeDtypeStruct((sectors, 2, half, cols), dtype)
    dma = pltpu.SemaphoreType.DMA
    first, second = pl.pallas_call(
        kernel,
        out_shape=(out, out),
        in_specs=[pl.BlockSpec(memory_space=pl.ANY)] * 3
        + [pl.BlockSpec(memory_space=pltpu.SMEM)] * 3,
        out_specs=[pl.BlockSpec(memory_space=pl.ANY)] * 2,
        scratch_shapes=[
            pltpu.VMEM((channels, rows, states), dtype),
            pltpu.VMEM((channels, bonds, 2, half, states), dtype),
            pltpu.VMEM((groups // 2, bonds, half, cols), dtype),
            pltpu.VMEM((2, groups, bonds, 2, half, cols), dtype),
            pltpu.VMEM((channels, rows, states), dtype),
            pltpu.VMEM((groups, rows, cols), jnp.float32),
            pltpu.VMEM((2, groups, rows, cols), dtype),
            pltpu.VMEM((2, 2, groups, y_rows, cols), dtype),
            pltpu.VMEM((groups, y_rows, cols), dtype),
            pltpu.VMEM((2, groups, y_rows, cols), dtype),
            pltpu.VMEM((groups, 3, z_rows, cols), dtype),
            pltpu.VMEM((2, groups, 3, z_rows, cols), dtype),
            pltpu.VMEM((2, z_rows, cols), dtype),
            pltpu.VMEM((2, 2, z_rows, cols), dtype),
            pltpu.VMEM((bonds, half, cols), dtype),
            dma((4,)),
            dma((2,)),
            dma((groups // 2,)),
            dma((1,)),
            dma((groups // 2,)),
            dma((1,)),
            dma((groups - 1, PIECES)),
            dma((groups // 2,)),
            dma((1,)),
            dma((2, groups, PIECES)),
            dma((2,)),
            dma((2, 2, groups)),
            dma((2,)),
            dma((2, groups)),
            dma((2, groups)),
            dma((2,)),
            dma((2, 2)),
            dma((2,)),
            dma((2,)),
        ],
        compiler_params=pltpu.CompilerParams(
            collective_id=0, has_side_effects=True, vmem_limit_bytes=56 << 20
        ),
        cost_estimate=pl.CostEstimate(
            flops=8 * channels * rows * states * states,
            bytes_accessed=6 * channels * rows * states,
            transcendentals=0,
        ),
        name="two_steps",
    )(
        wavefunction,
        left_env.reshape(channels, rows, states),
        right_env.reshape(channels, bonds, half, states),
        left_sizes,
        right_sizes,
        channel_shift,
    )
    first, second = pl.pallas_call(hand_over, out_shape=(out, out), name="hand_over")(
        first, second
    )
    shape = (sectors, block_rows, cols)
    return first.reshape(shape), second.reshape(shape)


def solution(mesh):
    placed = (
        P(None, "bond", None),
        P("mpo", "bond", None, None),
        P("mpo", "bond", None, None),
        P(),
        P(),
        P(),
    )
    return jax.shard_map(
        local,
        mesh=mesh,
        in_specs=placed,
        out_specs=(P(None, "bond", "mpo"), P(None, "bond", "mpo")),
        check_vma=False,
    )
```
